256 devices in a mesh: dp: 32 (over z, y), ctx: 8 (over x, core).
Axes of the slice: x: 4, y: 4, z: 8, core: 2. Of those that a mesh axis runs over, the one named last changes fastest.
Arguments:
- queries: bfloat16 [32768, 2048], P(('dp', 'ctx'))
- keys: bfloat16 [32768, 2048], P(('dp', 'ctx'))
- values: bfloat16 [32768, 2048], P(('dp', 'ctx')), may hold values from -6 to 6
- spans: int32 [32, 2], P('dp'), may hold values from 128 to 1023, as said below
- resid_in: bfloat16 [32768, 4096], P('dp'), may hold values from -2 to 2
- out_weight: bfloat16 [2048, 4096], P('ctx', 'dp'), may hold values from -0.375 to 0.375
- norm_gain: float32 [4096], replicated, may hold values from 0.1 to 1.9
- gate_weight: bfloat16 [4096, 5504], P('dp', 'ctx'), may hold values from -0.09375 to 0.09375
- up_weight: bfloat16 [4096, 5504], P('dp', 'ctx'), may hold values from -0.09375 to 0.09375
Outputs:
- resid_out: bfloat16 [32768, 4096], P(('dp', 'ctx'))
- hidden: bfloat16 [32768, 5504], P('dp', 'ctx')
The draws below stay inside these ranges and needn't reach their ends.
Inputs may be any that keep to these rules, and one draw needn't show every extreme that they name: `spans`: in each slab, 128 <= prefix end <= 512 and prefix end < middle end <= 1023.
All inputs are finite; a program needn't handle non-finite values.
Results may differ from the reference program's by a relative error of at most 0.025.
Values may be sent and summed in bfloat16 or wider, within the bound.
A program may use at most 128 MiB of HBM per device.

```python
import jax
import jax.numpy as jnp
from jax import lax

D = 4096
HEADS = 16
HEAD_DIM = 128
FF_WIN = 5504
SEQ = 1024
SLABS = 32
TOKENS = 32768
N_CTX = 8


def span_table(key):
    key_prefix, key_middle = jax.random.split(jax.random.fold_in(key, 11))
    lowest = SEQ // 8
    prefix_end = jax.random.randint(key_prefix, (SLABS,), lowest, SEQ // 2 + 1)
    spread = jax.random.randint(key_middle, (SLABS,), 0, 1 << 20)
    middle_end = prefix_end + 1 + spread % (SEQ - 1 - prefix_end)
    first = lax.iota(jnp.int32, SLABS) == 0
    prefix_end = jnp.where(first, lowest, prefix_end)
    middle_end = jnp.where(first, SEQ - 1, middle_end)
    return jnp.stack([prefix_end, middle_end], axis=1).astype(jnp.int32)


def draw_spans(key, part):
    return span_table(key)


def draw_queries(key, part):
    own_key = jax.random.fold_in(key, 1)
    result = jnp.clip(jax.random.normal(own_key, (TOKENS, HEADS * HEAD_DIM), jnp.float32), -6.0, 6.0)
    return result.astype(jnp.bfloat16)


def draw_keys(key, part):
    own_key = jax.random.fold_in(key, 2)
    result = jnp.clip(jax.random.normal(own_key, (TOKENS, HEADS * HEAD_DIM), jnp.float32), -6.0, 6.0)
    return result.astype(jnp.bfloat16)


def block_scale(rng, shape, cuts, low, high):
    level, own = 1.0, jax.random.fold_in(rng, 6)
    for position, parts in cuts:
        heights = jnp.exp(jax.random.uniform(jax.random.fold_in(own, position), (parts,), jnp.float32, low / len(cuts), high / len(cuts)))
        level = level * jnp.repeat(heights, shape[position] // parts).reshape([-1 if axis == position else 1 for axis in range(len(shape))])
    return level


def gaussian(key, dims, scale, bound, pieces=(), held_as=jnp.bfloat16):
    array = scale * jax.random.normal(key, dims, jnp.float32)
    if pieces:
        array = array * block_scale(key, dims, pieces, -0.22, 0.18)
    return jnp.clip(array, -bound, bound).astype(held_as)


def setup_inputs(seed: int = 0) -> dict:
    streams_of = jax.random.split(jax.random.key(seed), 10)
    queries = draw_queries(jax.random.fold_in(streams_of[9], 71), 0)
    keys = draw_keys(jax.random.fold_in(streams_of[9], 71), 0)
    values = gaussian(streams_of[2], (TOKENS, HEADS * HEAD_DIM), 1.0, 6.0, ((0, 256),))
    spans = draw_spans(jax.random.fold_in(streams_of[9], 71), 0)
    resid_in = gaussian(streams_of[4], (TOKENS, D), 0.3, 2.0, ((0, 32),))
    out_weight = gaussian(streams_of[5], (HEADS * HEAD_DIM, D), (HEADS * HEAD_DIM // 8) ** -0.5, 0.375, ((0, 8), (1, 32)))
    norm_gain = jnp.clip(1.0 + 0.18 * jax.random.normal(streams_of[6], (D,), jnp.float32), 0.1, 1.9)
    gate_weight = gaussian(streams_of[7], (D, FF_WIN), D ** -0.5, 0.09375, ((0, 32), (1, 8)))
    up_weight = gaussian(streams_of[8], (D, FF_WIN), D ** -0.5, 0.09375, ((0, 32), (1, 8)))
    return {"queries": queries, "keys": keys, "values": values, "spans": spans, "resid_in": resid_in, "out_weight": out_weight, "norm_gain": norm_gain, "gate_weight": gate_weight, "up_weight": up_weight}


def slab_ranks(prefix_end, middle_end, length):
    pos = lax.iota(jnp.int32, length)
    return jnp.where(pos < prefix_end, pos, jnp.where(pos >= middle_end, prefix_end + pos - middle_end, prefix_end + (length - middle_end) + (pos - prefix_end))).astype(jnp.int32)

def reference(queries, keys, values, spans, resid_in, out_weight, norm_gain, gate_weight, up_weight):
    width = HEADS * HEAD_DIM // N_CTX

    def one_slab(index):
        row0 = (index * SEQ).astype(jnp.int32)
        q_rows = lax.dynamic_slice_in_dim(queries, row0, SEQ, 0).reshape(SEQ, HEADS, HEAD_DIM).astype(jnp.float32)
        k_rows = lax.dynamic_slice_in_dim(keys, row0, SEQ, 0).reshape(SEQ, HEADS, HEAD_DIM).astype(jnp.float32)
        v_rows = lax.dynamic_slice_in_dim(values, row0, SEQ, 0).reshape(SEQ, HEADS, HEAD_DIM).astype(jnp.float32)
        rank = slab_ranks(spans[index, 0], spans[index, 1], SEQ)
        scores = jnp.einsum('qhd,khd->hqk', q_rows, k_rows) * (1.0 / jnp.sqrt(jnp.float32(HEAD_DIM)))
        allowed = rank[None, :, None] >= rank[None, None, :]
        scores = jnp.where(allowed, scores, jnp.float32(-1e+30))
        peak = lax.optimization_barrier(jnp.max(scores, axis=-1, keepdims=True))
        expo = jnp.where(allowed, jnp.exp(scores - peak), jnp.float32(0.0))
        probs = (expo / lax.optimization_barrier(jnp.sum(expo, axis=-1, keepdims=True))).astype(jnp.bfloat16)
        context = jnp.einsum('hqk,khd->qhd', probs.astype(jnp.float32), v_rows)
        context = context.astype(jnp.bfloat16).reshape(SEQ, HEADS * HEAD_DIM)
        attn_out = jnp.zeros((SEQ, D), jnp.float32)
        for group in range(N_CTX):
            part = jnp.dot(context[:, group * width:(group + 1) * width], out_weight[group * width:(group + 1) * width], preferred_element_type=jnp.float32)
            attn_out = attn_out + part.astype(jnp.bfloat16).astype(jnp.float32)
        stream = lax.dynamic_slice_in_dim(resid_in, row0, SEQ, 0).astype(jnp.float32) + attn_out
        scale = lax.rsqrt(lax.optimization_barrier(jnp.mean(stream * stream, axis=-1, keepdims=True)) + 1e-05)
        normed = (stream * scale * norm_gain).astype(jnp.bfloat16)
        gate = jnp.dot(normed, gate_weight, preferred_element_type=jnp.float32)
        up = jnp.dot(normed, up_weight, preferred_element_type=jnp.float32)
        hidden = (jax.nn.silu(gate) * up).astype(jnp.bfloat16)
        return (stream.astype(jnp.bfloat16), hidden)
    resid_out, hidden = lax.map(one_slab, lax.iota(jnp.int32, SLABS))
    return (resid_out.reshape(TOKENS, D), hidden.reshape(TOKENS, FF_WIN))
```

```python
import functools
import math

import jax
import jax.numpy as jnp
from jax import lax
from jax.experimental import pallas as pl
from jax.experimental.pallas import tpu as pltpu
from jax.sharding import PartitionSpec as P

MESH = pl.DeviceIdType.MESH
Z, Y, X = 8, 4, 4
HD = 128
SEQ, D, FF = 1024, 4096, 688
N_BLOCKS = FF // 128
TAIL = FF - 128 * N_BLOCKS
WIDE = 256 * N_BLOCKS + 128
PART_COLS = {"A": (0, 512), "B": (512, WIDE - 512)}
EXP2_SCALE = math.log2(math.e) / math.sqrt(HD)
F32, BF16 = jnp.float32, jnp.bfloat16
N_SEMS = 256


def mult(value, of):
    return pl.multiple_of(value, of)


def kernel(
    q_in, k_in, v_in, spans, resid, wo_in, gain, gate_in, up_in,
    resid_out, hidden,
    qkv, ctx_own, ctx_all, res, stream, wo, w, hid, out_rows,
    send_sem, recv_sem, local_sem,
):
    cx, dp = lax.axis_index("ctx"), lax.axis_index("dp")
    x, c = cx // 2, cx % 2
    z, y = dp // Y, dp % Y

    def dev(dz=0, dy=0, dx=0, dc=0):
        zz, yy = (z + dz + Z) % Z, (y + dy + Y) % Y
        xx, cc = (x + dx + X) % X, (c + dc) % 2
        return (zz * Y + yy, xx * 2 + cc)

    recv_ids, sent, state = {}, [], {"send": 0, "local": 0}

    def recv_id(key):
        return recv_ids.setdefault(key, len(recv_ids))

    def send(src, dst, target, key, when=None):
        index = state["send"]
        state["send"] += 1
        copy = pltpu.make_async_remote_copy(
            src_ref=src, dst_ref=dst, send_sem=send_sem.at[index], recv_sem=recv_sem.at[recv_id(key)],
            device_id=target, device_id_type=MESH,
        )
        copy.start()
        if when is None:
            sent.append(copy)
        return copy

    def recv(dst, key):
        pltpu.make_async_remote_copy(
            src_ref=dst, dst_ref=dst, send_sem=send_sem.at[0], recv_sem=recv_sem.at[recv_id(key)],
            device_id=dev(0, 0, 0, 1), device_id_type=MESH,
        ).wait_recv()

    def local(src, dst):
        copy = pltpu.make_async_copy(src, dst, local_sem.at[state["local"]])
        state["local"] += 1
        copy.start()
        return copy

    barrier = pltpu.get_barrier_semaphore()
    peers = [(0, 0, dx, dc) for dx in range(X) for dc in range(2) if (dx, dc) != (0, 0)]
    peers += [(0, 1, 0, 0), (0, 2, 0, 0), (0, 3, 0, 0), (1, 0, 0, 0), (-1, 0, 0, 0)]
    for peer in peers:
        pl.semaphore_signal(barrier, inc=1, device_id=dev(*peer), device_id_type=MESH)
    pl.semaphore_wait(barrier, len(peers))

    mine = pl.ds(mult(cx * 128, 128), 128)
    shares = [(1, k_in), (2, v_in), (0, q_in)]
    order = [(dx, dc) for dx in (2, 1, 3, 0) for dc in range(2) if (dx, dc) != (0, 0)]
    for which, source in shares:
        for dx, dc in order:
            target = dev(0, 0, dx, dc)
            columns = pl.ds(mult(target[1] * 256, 256), 256)
            send(source.at[:, columns], qkv.at[which, mine], target, ("qkv", which, dx, dc))
    own_columns = pl.ds(mult(cx * 256, 256), 256)
    loads = [local(source.at[:, own_columns], qkv.at[which, mine]) for which, source in shares]
    res_loads = []
    for zz in range(Z):
        columns = pl.ds(mult(zz * 512 + x * 128, 128), 128)
        res_loads.append(local(resid.at[:, c, :, columns], res.at[:, :, pl.ds(zz * 128, 128)]))

    def wo_block(zz, cc, half=None):
        rows = pl.ds(mult(cc * 1024, 1024), 1024) if half is None else pl.ds(mult(cc * 1024 + half * 512, 512), 512)
        return wo.at[rows, pl.ds(mult(zz * 128, 128), 128)]

    def wo_rows(xx):
        return wo.at[pl.ds(mult(c * 1024 + xx * 256, 256), 256), pl.ds(mult(z * 128, 128), 128)]

    collector = x == y
    gather = {}
    wo_first = state["send"]
    state["send"] += 4
    for ahead in range(1, X):
        gather[ahead] = pltpu.make_async_remote_copy(
            src_ref=wo_in, dst_ref=wo_rows(x), send_sem=send_sem.at[wo_first],
            recv_sem=recv_sem.at[recv_id(("wo_x", ahead))], device_id=dev(0, 0, ahead, 0), device_id_type=MESH,
        )

        @pl.when((x + ahead) % X == y)
        def _(copy=gather[ahead]):
            copy.start()

    diagonal = lax.broadcasted_iota(jnp.int32, (128, 128), 0) == lax.broadcasted_iota(jnp.int32, (128, 128), 1)
    gain_row = gain[pl.ds(dp, 1), :]
    gain_column = jnp.sum(jnp.where(diagonal, gain_row, 0.0), axis=1, keepdims=True)

    def w_rows(zz, yy, half=None):
        start = (yy % Y) * 1024 + (zz % Z) * 128
        return pl.ds(mult(start, 128), 128) if half is None else pl.ds(mult(start + half * 64, 64), 64)

    own = w_rows(z, y)
    for block in range(N_BLOCKS):
        at = 256 * block
        w[own, at : at + 128] = (gate_in[:, 128 * block : 128 * block + 128].astype(F32) * gain_column).astype(BF16)
        w[own, at + 128 : at + 256] = (up_in[:, 128 * block : 128 * block + 128].astype(F32) * gain_column).astype(BF16)
    tails = jnp.concatenate(
        [gate_in[:, 128 * N_BLOCKS :].astype(F32), up_in[:, 128 * N_BLOCKS :].astype(F32), jnp.zeros((128, 128 - 2 * TAIL), F32)],
        axis=1,
    )
    w[own, 256 * N_BLOCKS :] = (tails * gain_column).astype(BF16)

    def w_block(part, dz, dy, half=None):
        first, count = PART_COLS[part]
        return w.at[w_rows(z + dz + Z, y + dy + Y, half), first : first + count]

    def z_send(part, dz, dy, d, key, half=None):
        ref = w_block(part, dz, dy, half)
        send(ref, ref, dev(d, 0, 0, 0), key)

    def y_send(part, dz, dy, d, key, half=None):
        ref = w_block(part, dz, dy, half)
        send(ref, ref, dev(0, d, 0, 0), key)

    def z_start(part, dy):
        for d in (1, -1):
            z_send(part, 0, dy, d, (part, "z", dy, d, 1))

    def z_wait(part, dy, hop):
        for d in (1, -1):
            half = None if hop < 4 else (0 if d == 1 else 1)
            recv(w_block(part, -d * hop, dy, half), (part, "z", dy, d, hop))

    def z_pass(part, dy, hop):
        for d in (1, -1):
            half = None if hop < 3 else (0 if d == 1 else 1)
            z_send(part, -d * hop, dy, d, (part, "z", dy, d, hop + 1), half)

    def z_event(part, dy, hop):
        z_wait(part, dy, hop)
        if hop < 4:
            z_pass(part, dy, hop)

    def y_start(part, dz):
        for d in (1, -1):
            y_send(part, dz, 0, d, (part, "y", dz, d, 1))

    def y_event(part, dz, hop):
        for d in (1, -1):
            half = None if hop < 2 else (0 if d == 1 else 1)
            recv(w_block(part, dz, -d * hop, half), (part, "y", dz, d, hop))
            if hop == 1:
                half = 0 if d == 1 else 1
                y_send(part, dz, -d, d, (part, "y", dz, d, 2), half)

    y_start("A", 0)
    z_start("B", 0)
    z_start("A", 0)
    y_start("B", 0)

    @pl.when(collector)
    def _():
        for ahead in range(1, X):
            recv(wo_rows((x - ahead + X) % X), ("wo_x", ahead))
        wo[pl.ds(mult(c * 1024 + x * 256, 256), 256), pl.ds(mult(z * 128, 128), 128)] = wo_in[...]

    spread = []
    for ahead in range(1, Y):
        spread.append(
            pltpu.make_async_remote_copy(
                src_ref=wo_block(z, c), dst_ref=wo_block(z, c), send_sem=send_sem.at[wo_first + ahead],
                recv_sem=recv_sem.at[recv_id("wo_y")], device_id=dev(0, ahead, 0, 0), device_id_type=MESH,
            )
        )

        @pl.when(collector)
        def _(copy=spread[-1]):
            copy.start()

    y_event("A", 0, 1)
    z_start("A", -1)

    @pl.when(jnp.logical_not(collector))
    def _():
        recv(wo_block(z, c), "wo_y")

    def wo_across(dz, half=None):
        ref = wo_block((z + dz + Z) % Z, c, half)
        send(ref, ref, dev(0, 0, 0, 1), ("wo_d", dz, half))

    def wo_event(hop):
        for d in (1, -1):
            half = None if hop < 4 else (0 if d == 1 else 1)
            ref = wo_block((z - d * hop + Z) % Z, c, half)
            recv(ref, ("wo_z", d, hop))
            if hop < 4:
                half_on = None if hop < 3 else (0 if d == 1 else 1)
                ref = wo_block((z - d * hop + Z) % Z, c, half_on)
                send(ref, ref, dev(d, 0, 0, 0), ("wo_z", d, hop + 1))
            wo_across(4 if hop == 4 else -d * hop, half)

    for d in (1, -1):
        ref = wo_block(z, c)
        send(ref, ref, dev(d, 0, 0, 0), ("wo_z", d, 1))
    wo_across(0)
    y_event("A", 0, 2)
    z_wait("B", 0, 1)
    y_start("B", 1)
    y_start("B", -1)
    wo_event(1)

    for copy in loads:
        copy.wait()
    for which, _ in shares:
        for dx, dc in order:
            rows = pl.ds(mult(dev(0, 0, -dx, dc)[1] * 128, 128), 128)
            recv(qkv.at[which, rows], ("qkv", which, dx, dc))

    prefix_end, middle_end = spans[0, 0], spans[0, 1]

    def ranks(pos):
        late = prefix_end + (SEQ - middle_end) + (pos - prefix_end)
        return jnp.where(pos < prefix_end, pos, jnp.where(pos >= middle_end, prefix_end + pos - middle_end, late))

    key_rank = ranks(lax.broadcasted_iota(jnp.int32, (1, SEQ), 1))

    def ctx_spot(k, cc, xx, half=None):
        rows = pl.ds(128 * k, 128) if half is None else pl.ds(128 * k + 64 * half, 64)
        return ctx_all.at[rows, pl.ds(mult(cc * 1024 + xx * 256, 256), 256)]

    def attend(k, rel):
        row = mult((2 * k + (c + rel) % 2) * 128, 128)
        rows = pl.ds(row, 128)
        query_rank = ranks(row + lax.broadcasted_iota(jnp.int32, (128, 1), 0))
        allowed = query_rank >= key_rank
        for head in range(2):
            cols = slice(head * HD, head * HD + HD)
            scores = lax.dot_general(
                qkv[0, rows, cols], qkv[1, :, cols], (((1,), (1,)), ((), ())), preferred_element_type=F32
            )
            scores = jnp.where(allowed, scores, -jnp.inf)
            peak = jnp.max(scores, axis=1, keepdims=True)
            expo = jnp.exp2((scores - peak) * EXP2_SCALE)
            total = jnp.sum(expo, axis=1, keepdims=True)
            mixed = jnp.dot(expo.astype(BF16), qkv[2, :, cols], preferred_element_type=F32)
            mixed = (mixed / total).astype(BF16)
            ctx_own[rows, cols] = mixed
            if rel == 0:
                ctx_all[128 * k : 128 * k + 128, pl.ds(mult(c * 1024 + x * 256 + head * HD, 128), HD)] = mixed
        for d in (1, -1):
            send(ctx_own.at[rows], ctx_spot(k, c, x), dev(0, 0, d, rel), ("ctx", k, rel, d, 1))
        if rel == 1:
            send(ctx_own.at[rows], ctx_spot(k, c, x), dev(0, 0, 0, 1), ("ctx_d", k))

    def ctx_pass(k):
        for rel in range(2):
            cc = (c + rel) % 2
            for d in (1, -1):
                recv(ctx_spot(k, cc, (x - d + X) % X), ("ctx", k, rel, d, 1))
                ref = ctx_spot(k, cc, (x - d + X) % X, 0 if d == 1 else 1)
                send(ref, ref, dev(0, 0, d, 0), ("ctx", k, rel, d, 2))

    def ctx_end(k):
        recv(ctx_spot(k, (c + 1) % 2, x), ("ctx_d", k))
        for rel in range(2):
            for d in (1, -1):
                recv(ctx_spot(k, (c + rel) % 2, (x + 2) % X, 0 if d == 1 else 1), ("ctx", k, rel, d, 2))

    for k in range(2):
        for rel in (1, 0):
            attend(k, rel)
    wo_event(2)
    y_event("B", 0, 1)
    for k in range(2, 4):
        for rel in (1, 0):
            attend(k, rel)
    wo_event(3)
    z_pass("B", 0, 1)
    z_event("A", 0, 1)
    z_start("A", 1)
    z_start("A", 2)
    ctx_pass(0)
    ctx_pass(1)
    z_event("A", -1, 1)
    wo_event(4)

    def stream_spot(k, cc, xx, half=None):
        row = (2 * k + cc) * 128
        rows = pl.ds(mult(row, 128), 128) if half is None else pl.ds(mult(row + half * 64, 64), 64)
        return stream.at[rows, pl.ds(mult(xx * 1024, 1024), 1024)]

    def project(k):
        rows = pl.ds(mult((2 * k + c) * 128, 128), 128)
        for block in range(4):
            part = jnp.dot(
                ctx_all[128 * k : 128 * k + 128, :], wo[:, 256 * block : 256 * block + 256], preferred_element_type=F32
            )
            part = part + res[k, :, 256 * block : 256 * block + 256].astype(F32)
            stream[rows, pl.ds(mult(x * 1024 + 256 * block, 256), 256)] = part.astype(BF16)
        ref = stream_spot(k, c, x)
        for d in (1, -1):
            send(ref, ref, dev(0, 0, d, 0), ("st", k, d, 1))
        send(ref, ref, dev(0, 0, 0, 1), ("st_d", k, 0, 0))

    def stream_pass(k, hop):
        for d in (1, -1):
            half = None if hop == 1 else (0 if d == 1 else 1)
            ref = stream_spot(k, c, (x - d * hop + X) % X, half)
            recv(ref, ("st", k, d, hop))
            if hop == 1:
                on = stream_spot(k, c, (x - d + X) % X, 0 if d == 1 else 1)
                send(on, on, dev(0, 0, d, 0), ("st", k, d, 2))
            send(ref, ref, dev(0, 0, 0, 1), ("st_d", k, d, hop))

    def stream_end(k):
        other = (c + 1) % 2
        recv(stream_spot(k, other, x), ("st_d", k, 0, 0))
        for hop in (1, 2):
            for d in (1, -1):
                half = None if hop == 1 else (0 if d == 1 else 1)
                recv(stream_spot(k, other, (x - d * hop + X) % X, half), ("st_d", k, d, hop))

    for dz, half in [(0, None), (-1, None), (1, None), (-2, None), (2, None), (-3, None), (3, None), (4, 0), (4, 1)]:
        recv(wo_block((z + dz + Z) % Z, (c + 1) % 2, half), ("wo_d", dz, half))
    for copy in res_loads:
        copy.wait()
    ctx_end(0)
    project(0)
    ctx_pass(2)
    ctx_end(1)
    project(1)
    ctx_pass(3)
    y_event("B", 0, 2)
    y_event("B", -1, 1)
    y_event("B", 1, 1)
    z_wait("B", 0, 2)
    z_pass("B", 0, 2)
    y_start("B", 2)
    y_start("B", -2)
    ctx_end(2)
    project(2)
    z_event("A", 0, 2)
    z_event("A", 1, 1)
    stream_pass(0, 1)
    ctx_end(3)
    project(3)
    z_event("A", 2, 1)
    z_event("A", -1, 2)
    y_event("B", -1, 2)
    y_event("B", 1, 2)
    stream_pass(1, 1)
    stream_pass(0, 2)
    z_event("B", 0, 3)
    y_start("B", 3)
    y_start("B", -3)
    z_event("A", 0, 3)
    z_event("A", 1, 2)
    z_event("A", 2, 2)
    y_event("B", 2, 1)
    y_event("B", -2, 1)
    stream_pass(2, 1)
    stream_pass(1, 2)
    z_event("A", -1, 3)
    z_event("B", 0, 4)
    y_start("B", 4)
    z_event("A", 1, 3)
    z_event("A", 2, 3)
    stream_pass(3, 1)
    stream_pass(2, 2)
    y_event("B", 2, 2)
    y_event("B", -2, 2)
    y_event("B", 3, 1)
    y_event("B", -3, 1)
    y_event("B", 4, 1)
    y_event("B", 3, 2)
    y_event("B", -3, 2)
    for dy in (0, -1, 1, 2):
        z_event("A", dy, 4)
    y_event("B", 4, 2)
    stream_pass(3, 2)

    outs = []

    def feed_forward(k):
        rows = pl.ds(256 * k, 256)

        def add_squares(i, total):
            piece = stream[rows, pl.ds(mult(i * 256, 256), 256)].astype(F32)
            piece = piece * piece
            return total + piece[:, :128] + piece[:, 128:]

        squares = lax.fori_loop(0, D // 256, add_squares, jnp.zeros((256, 128), F32))
        scale = lax.rsqrt(jnp.sum(squares, axis=1, keepdims=True) * (1.0 / D) + 1e-5)

        def one(block, _):
            both = jnp.dot(
                stream[rows, :], w[:, pl.ds(mult(block * 256, 256), 256)], preferred_element_type=F32
            )
            gate, up = both[:, :128] * scale, both[:, 128:] * scale
            hid[rows, pl.ds(mult(block * 128, 128), 128)] = (gate / (1.0 + jnp.exp(-gate)) * up).astype(BF16)
            return 0

        lax.fori_loop(0, N_BLOCKS, one, 0)
        both = jnp.dot(stream[rows, :], w[:, 256 * N_BLOCKS :], preferred_element_type=F32) * scale
        up = pltpu.roll(both, 128 - TAIL, 1)
        act = (both / (1.0 + jnp.exp(-both)) * up).astype(BF16)
        hid[rows, 128 * N_BLOCKS :] = act[:, :TAIL]
        outs.append(local(hid.at[rows], hidden.at[rows]))

    for k in range(4):
        stream_end(k)
        feed_forward(k)
    for yy in range(Y):
        for zz in range(Z):
            out_rows[:, zz * 512 + yy * 128 : zz * 512 + yy * 128 + 128] = stream[
                mine, yy * 1024 + zz * 128 : yy * 1024 + zz * 128 + 128
            ]
    outs.append(local(out_rows, resid_out))
    for copy in outs:
        copy.wait()
    for ahead in range(1, X):

        @pl.when((x + ahead) % X == y)
        def _(copy=gather[ahead]):
            copy.wait_send()

    @pl.when(collector)
    def _():
        for copy in spread:
            copy.wait_send()

    for copy in sent:
        copy.wait_send()
    assert state["send"] <= N_SEMS and len(recv_ids) <= N_SEMS


def body(queries, keys, values, spans, resid_in, out_weight, norm_gain, gate_weight, up_weight):
    anywhere = pl.BlockSpec(memory_space=pl.ANY)
    vmem = pl.BlockSpec(memory_space=pltpu.VMEM)
    smem = pl.BlockSpec(memory_space=pltpu.SMEM)
    return pl.pallas_call(
        kernel,
        out_shape=(jax.ShapeDtypeStruct((128, D), BF16), jax.ShapeDtypeStruct((SEQ, FF), BF16)),
        in_specs=[anywhere, anywhere, anywhere, smem, anywhere, vmem, vmem, vmem, vmem],
        out_specs=(anywhere, anywhere),
        scratch_shapes=[
            pltpu.VMEM((3, SEQ, 256), BF16),
            pltpu.VMEM((SEQ, 256), BF16),
            pltpu.VMEM((512, 2048), BF16),
            pltpu.VMEM((4, 128, 1024), BF16),
            pltpu.VMEM((SEQ, D), BF16),
            pltpu.VMEM((2048, 1024), BF16),
            pltpu.VMEM((D, WIDE), BF16),
            pltpu.VMEM((SEQ, FF), BF16),
            pltpu.VMEM((128, D), BF16),
            pltpu.SemaphoreType.DMA((N_SEMS,)),
            pltpu.SemaphoreType.DMA((N_SEMS,)),
            pltpu.SemaphoreType.DMA((32,)),
        ],
        compiler_params=pltpu.CompilerParams(
            collective_id=0, has_side_effects=True, vmem_limit_bytes=56 * 1024 * 1024
        ),
    )(
        queries, keys, values, spans, resid_in.reshape(4, 2, 128, D), out_weight,
        norm_gain.reshape(D // 128, 128), gate_weight, up_weight,
    )


def solution(mesh):
    return jax.shard_map(
        body,
        mesh=mesh,
        in_specs=(
            P(("dp", "ctx"), None),
            P(("dp", "ctx"), None),
            P(("dp", "ctx"), None),
            P("dp", None),
            P("dp", None),
            P("ctx", "dp"),
            P(),
            P("dp", "ctx"),
            P("dp", "ctx"),
        ),
        out_specs=(P(("dp", "ctx"), None), P("dp", "ctx")),
        check_vma=False,
    )
```

```python
import functools
import math

import jax
import jax.numpy as jnp
from jax import lax
from jax.experimental import pallas as pl
from jax.experimental.pallas import tpu as pltpu
from jax.sharding import PartitionSpec as P

MESH = pl.DeviceIdType.MESH
Z, Y, X = 8, 4, 4
HD = 128
SEQ, D, FF = 1024, 4096, 688
PART_ROWS = {"A": (0, 512), "B": (512, 2 * FF - 512)}
EXP2_SCALE = math.log2(math.e) / math.sqrt(HD)
F32, BF16 = jnp.float32, jnp.bfloat16
N_SEMS = 256


def mult(value, of):
    return pl.multiple_of(value, of)


def kernel(
    q_in, k_in, v_in, spans, resid, wo_in, gain, gate_in, up_in,
    resid_out, hidden,
    qkv, ctx_own, ctx_all, res, stream, wo, w, acc, scales, hid,
    send_sem, recv_sem, local_sem,
):
    cx, dp = lax.axis_index("ctx"), lax.axis_index("dp")
    x, c = cx // 2, cx % 2
    z, y = dp // Y, dp % Y

    def dev(dz=0, dy=0, dx=0, dc=0):
        zz, yy = (z + dz + Z) % Z, (y + dy + Y) % Y
        xx, cc = (x + dx + X) % X, (c + dc) % 2
        return (zz * Y + yy, xx * 2 + cc)

    recv_ids, sent, state = {}, [], {"send": 0, "local": 0, "drained": 0}

    def recv_id(key):
        return recv_ids.setdefault(key, len(recv_ids))

    def send(src, dst, target, key, when=None):
        index = state["send"]
        state["send"] += 1
        copy = pltpu.make_async_remote_copy(
            src_ref=src, dst_ref=dst, send_sem=send_sem.at[index], recv_sem=recv_sem.at[recv_id(key)],
            device_id=target, device_id_type=MESH,
        )
        copy.start()
        if when is None:
            sent.append(copy)
        return copy

    def recv(dst, key):
        pltpu.make_async_remote_copy(
            src_ref=dst, dst_ref=dst, send_sem=send_sem.at[0], recv_sem=recv_sem.at[recv_id(key)],
            device_id=dev(0, 0, 0, 1), device_id_type=MESH,
        ).wait_recv()

    def drain(count):
        for copy in sent[state["drained"] : count]:
            copy.wait_send()
        state["drained"] = max(count, state["drained"])

    def local(src, dst):
        copy = pltpu.make_async_copy(src, dst, local_sem.at[state["local"]])
        state["local"] += 1
        copy.start()
        return copy

    barrier = pltpu.get_barrier_semaphore()
    peers = [(0, 0, dx, dc) for dx in range(X) for dc in range(2) if (dx, dc) != (0, 0)]
    peers += [(0, 1, 0, 0), (0, 2, 0, 0), (0, 3, 0, 0), (1, 0, 0, 0), (-1, 0, 0, 0)]
    for peer in peers:
        pl.semaphore_signal(barrier, inc=1, device_id=dev(*peer), device_id_type=MESH)
    pl.semaphore_wait(barrier, len(peers))

    def wo_block(zz, cc, unit=None):
        rows = pl.ds(mult(cc * 1024, 1024), 1024) if unit is None else pl.ds(mult(cc * 1024 + unit * 512, 512), 512)
        return wo.at[rows, pl.ds(mult((zz + Z) % Z * 128, 128), 128)]

    def wo_rows(xx):
        return wo.at[pl.ds(mult(c * 1024 + xx * 256, 256), 256), pl.ds(mult(z * 128, 128), 128)]

    collector = x == y
    gather = {}
    wo_first = state["send"]
    state["send"] += 7
    for ahead in range(1, X):
        gather[ahead] = pltpu.make_async_remote_copy(
            src_ref=wo_in, dst_ref=wo_rows(x), send_sem=send_sem.at[wo_first],
            recv_sem=recv_sem.at[recv_id(("wo_x", ahead))], device_id=dev(0, 0, ahead, 0), device_id_type=MESH,
        )

        @pl.when((x + ahead) % X == y)
        def _(copy=gather[ahead]):
            copy.start()

    mine = pl.ds(mult(cx * 128, 128), 128)
    shares = [(1, k_in), (2, v_in), (0, q_in)]
    order = [(dx, dc) for dx in (2, 1, 3, 0) for dc in range(2) if (dx, dc) != (0, 0)]
    for which, source in shares:
        for dx, dc in order:
            target = dev(0, 0, dx, dc)
            columns = pl.ds(mult(target[1] * 256, 256), 256)
            send(source.at[:, columns], qkv.at[which, mine], target, ("qkv", which, dx, dc))
    own_columns = pl.ds(mult(cx * 256, 256), 256)
    loads = [local(source.at[:, own_columns], qkv.at[which, mine]) for which, source in shares]

    def pack_own():
        gain_row = gain[pl.ds(dp, 1), :]
        columns = pl.ds(mult(y * 128, 128), 128)
        w[z, :FF, columns] = (gate_in[...].astype(F32) * gain_row).astype(BF16)
        w[z, FF:, columns] = (up_in[...].astype(F32) * gain_row).astype(BF16)

    pack_own()

    def w_block(part, dz, dy, half=None):
        first, count = PART_ROWS[part]
        if half is not None:
            first, count = first + half * count // 2, count // 2
        return w.at[(z + dz + Z) % Z, first : first + count, pl.ds(mult((y + dy + Y) % Y * 128, 128), 128)]

    def z_send(part, dz, dy, d, key, half=None):
        ref = w_block(part, dz, dy, half)
        send(ref, ref, dev(d, 0, 0, 0), key)

    def y_send(part, dz, dy, d, key, half=None):
        ref = w_block(part, dz, dy, half)
        send(ref, ref, dev(0, d, 0, 0), key)

    def z_start(part, dy):
        for d in (1, -1):
            z_send(part, 0, dy, d, (part, "z", dy, d, 1))

    def z_wait(part, dy, hop):
        for d in (1, -1):
            half = None if hop < 4 else (0 if d == 1 else 1)
            recv(w_block(part, -d * hop, dy, half), (part, "z", dy, d, hop))

    def z_pass(part, dy, hop):
        for d in (1, -1):
            half = None if hop < 3 else (0 if d == 1 else 1)
            z_send(part, -d * hop, dy, d, (part, "z", dy, d, hop + 1), half)

    def z_event(part, dy, hop):
        z_wait(part, dy, hop)
        if hop < 4:
            z_pass(part, dy, hop)

    def y_start(part, dz):
        for d in (1, -1):
            y_send(part, dz, 0, d, (part, "y", dz, d, 1))

    def y_event(part, dz, hop):
        for d in (1, -1):
            half = None if hop < 2 else (0 if d == 1 else 1)
            recv(w_block(part, dz, -d * hop, half), (part, "y", dz, d, hop))
            if hop == 1:
                half = 0 if d == 1 else 1
                y_send(part, dz, -d, d, (part, "y", dz, d, 2), half)

    z_start("B", 0)
    z_start("A", 0)

    @pl.when(collector)
    def _():
        for ahead in range(1, X):
            recv(wo_rows((x - ahead + X) % X), ("wo_x", ahead))
        wo[pl.ds(mult(c * 1024 + x * 256, 256), 256), pl.ds(mult(z * 128, 128), 128)] = wo_in[...]

    spread = []
    for unit in range(2):
        for ahead in range(1, Y):
            spread.append(
                pltpu.make_async_remote_copy(
                    src_ref=wo_block(z, c, unit), dst_ref=wo_block(z, c, unit),
                    send_sem=send_sem.at[wo_first + 1 + len(spread)], recv_sem=recv_sem.at[recv_id(("wo_y", unit))],
                    device_id=dev(0, ahead, 0, 0), device_id_type=MESH,
                )
            )

            @pl.when(collector)
            def _(copy=spread[-1]):
                copy.start()

    def wo_y_wait(unit):
        @pl.when(jnp.logical_not(collector))
        def _():
            recv(wo_block(z, c, unit), ("wo_y", unit))

    def wo_across(dz, unit):
        ref = wo_block(z + dz, c, unit)
        send(ref, ref, dev(0, 0, 0, 1), ("wo_d", dz, unit))

    def wo_start(unit):
        ref = wo_block(z, c, unit)
        for d in (1, -1):
            send(ref, ref, dev(d, 0, 0, 0), ("wo_z", unit, d, 1))
        wo_across(0, unit)

    def wo_event(unit, hop):
        for d in (1, -1):
            if hop == 4 and unit != (0 if d == 1 else 1):
                continue
            ref = wo_block(z - d * hop, c, unit)
            recv(ref, ("wo_z", unit, d, hop))
            if hop < 3 or (hop == 3 and unit == (0 if d == 1 else 1)):
                send(ref, ref, dev(d, 0, 0, 0), ("wo_z", unit, d, hop + 1))
            wo_across(4 if hop == 4 else -d * hop, unit)

    def wo_d_wait():
        for dz in (0, -1, 1, -2, 2, -3, 3, 4):
            for unit in range(2):
                recv(wo_block(z + dz, (c + 1) % 2, unit), ("wo_d", dz, unit))

    def qkv_wait():
        for copy in loads:
            copy.wait()
        for which, _ in shares:
            for dx, dc in order:
                rows = pl.ds(mult(dev(0, 0, -dx, dc)[1] * 128, 128), 128)
                recv(qkv.at[which, rows], ("qkv", which, dx, dc))

    prefix_end, middle_end = spans[0, 0], spans[0, 1]

    def ranks(pos):
        late = prefix_end + (SEQ - middle_end) + (pos - prefix_end)
        return jnp.where(pos < prefix_end, pos, jnp.where(pos >= middle_end, prefix_end + pos - middle_end, late))

    key_rank = ranks(lax.broadcasted_iota(jnp.int32, (1, SEQ), 1))

    def ctx_spot(k, cc, xx, half=None):
        rows = pl.ds(128 * k, 128) if half is None else pl.ds(128 * k + 64 * half, 64)
        return ctx_all.at[rows, pl.ds(mult(cc * 1024 + xx * 256, 256), 256)]

    def attend(k, rel):
        row = mult((2 * k + (c + rel) % 2) * 128, 128)
        rows = pl.ds(row, 128)
        query_rank = ranks(row + lax.broadcasted_iota(jnp.int32, (128, 1), 0))
        allowed = query_rank >= key_rank
        for head in range(2):
            cols = slice(head * HD, head * HD + HD)
            scores = lax.dot_general(
                qkv[0, rows, cols], qkv[1, :, cols], (((1,), (1,)), ((), ())), preferred_element_type=F32
            )
            scores = jnp.where(allowed, scores, -jnp.inf)
            peak = jnp.max(scores, axis=1, keepdims=True)
            expo = jnp.exp2((scores - peak) * EXP2_SCALE)
            total = jnp.sum(expo, axis=1, keepdims=True)
            mixed = jnp.dot(expo.astype(BF16), qkv[2, :, cols], preferred_element_type=F32)
            mixed = (mixed / total).astype(BF16)
            ctx_own[rows, cols] = mixed
            if rel == 0:
                ctx_all[128 * k : 128 * k + 128, pl.ds(mult(c * 1024 + x * 256 + head * HD, 128), HD)] = mixed
        for d in (1, -1):
            send(ctx_own.at[rows], ctx_spot(k, c, x), dev(0, 0, d, rel), ("ctx", k, rel, d, 1))
        if rel == 1:
            send(ctx_own.at[rows], ctx_spot(k, c, x), dev(0, 0, 0, 1), ("ctx_d", k))

    def ctx_pass(k):
        for rel in range(2):
            cc = (c + rel) % 2
            for d in (1, -1):
                recv(ctx_spot(k, cc, (x - d + X) % X), ("ctx", k, rel, d, 1))
                ref = ctx_spot(k, cc, (x - d + X) % X, 0 if d == 1 else 1)
                send(ref, ref, dev(0, 0, d, 0), ("ctx", k, rel, d, 2))

    def ctx_end(k):
        recv(ctx_spot(k, (c + 1) % 2, x), ("ctx_d", k))
        for rel in range(2):
            for d in (1, -1):
                recv(ctx_spot(k, (c + rel) % 2, (x + 2) % X, 0 if d == 1 else 1), ("ctx", k, rel, d, 2))

    res_loads = []
    for zz in range(Z):
        columns = pl.ds(mult(zz * 512 + x * 128, 128), 128)
        res_loads.append(local(resid.at[:, c, :, columns], res.at[:, :, pl.ds(zz * 128, 128)]))

    def stream_spot(k, cc, xx, half=None):
        row = (2 * k + cc) * 128
        rows = pl.ds(mult(row, 128), 128) if half is None else pl.ds(mult(row + half * 64, 64), 64)
        return stream.at[:, rows, pl.ds(mult(xx * 128, 128), 128)]

    def project(k):
        rows = pl.ds(mult((2 * k + c) * 128, 128), 128)
        columns = pl.ds(mult(x * 128, 128), 128)
        for block in range(4):
            part = jnp.dot(
                ctx_all[128 * k : 128 * k + 128, :], wo[:, 256 * block : 256 * block + 256], preferred_element_type=F32
            )
            part = part + res[k, :, 256 * block : 256 * block + 256].astype(F32)
            stream[2 * block, rows, columns] = part[:, :128].astype(BF16)
            stream[2 * block + 1, rows, columns] = part[:, 128:].astype(BF16)
        ref = stream_spot(k, c, x)
        for d in (1, -1):
            send(ref, ref, dev(0, 0, d, 0), ("st", k, d, 1))
        send(ref, ref, dev(0, 0, 0, 1), ("st_d", k, 0, 0))

    def stream_pass(k, hop):
        for d in (1, -1):
            half = None if hop == 1 else (0 if d == 1 else 1)
            ref = stream_spot(k, c, (x - d * hop + X) % X, half)
            recv(ref, ("st", k, d, hop))
            if hop == 1:
                on = stream_spot(k, c, (x - d + X) % X, 0 if d == 1 else 1)
                send(on, on, dev(0, 0, d, 0), ("st", k, d, 2))
            send(ref, ref, dev(0, 0, 0, 1), ("st_d", k, d, hop))

    def stream_end(k):
        other = (c + 1) % 2
        recv(stream_spot(k, other, x), ("st_d", k, 0, 0))
        for hop in (1, 2):
            for d in (1, -1):
                half = None if hop == 1 else (0 if d == 1 else 1)
                recv(stream_spot(k, other, (x - d * hop + X) % X, half), ("st_d", k, d, hop))

    outs = []

    def norm_scale(k):
        rows = pl.ds(256 * k, 256)

        def add_squares(i, total):
            piece = stream[i, rows, :].astype(F32)
            piece = piece * piece
            return total + (piece[:, :128] + piece[:, 128:256]) + (piece[:, 256:384] + piece[:, 384:])

        squares = lax.fori_loop(0, Z, add_squares, jnp.zeros((256, 128), F32))
        total = jnp.sum(squares.T, axis=0, keepdims=True)
        scales[k] = lax.rsqrt(total * (1.0 / D) + 1e-5)

    def ff_part(k, *dzs):
        rows = slice(256 * k, 256 * k + 256)

        def one(half, _):
            at = pl.ds(mult(half * FF, 16), FF)
            total = None
            for dz in dzs:
                zz = (z + dz + Z) % Z
                part = lax.dot_general(
                    w[zz, at, :], stream[zz, rows, :], (((1,), (1,)), ((), ())), preferred_element_type=F32
                )
                total = part if total is None else total + part
            acc[at, rows] = total if 0 in dzs else acc[at, rows] + total
            return 0

        lax.fori_loop(0, 2, one, 0)

    def activate(k):
        rows = slice(256 * k, 256 * k + 256)
        scale = scales[k]
        for first in range(0, FF, 128):
            count = min(128, FF - first)
            gate = acc[first : first + count, rows] * scale
            up = acc[FF + first : FF + first + count, rows] * scale
            hid[first : first + count, rows] = (gate / (1.0 + jnp.exp(-gate)) * up).astype(BF16)
        outs.append(local(hid.at[:, rows], hidden.at[:, rows]))

    y_start("A", 0)
    y_event("A", 0, 1)
    z_start("A", -1)
    for unit in range(2):
        wo_y_wait(unit)
        wo_start(unit)
    y_start("B", 0)
    y_event("A", 0, 2)
    z_wait("B", 0, 1)
    y_start("B", 1)
    y_start("B", -1)
    wo_event(0, 1)
    wo_event(1, 1)
    qkv_wait()
    attend(0, 1)
    attend(0, 0)
    wo_event(0, 2)
    attend(1, 1)
    attend(1, 0)
    wo_event(1, 2)
    attend(2, 1)
    attend(2, 0)
    attend(3, 1)
    attend(3, 0)
    wo_event(0, 3)
    ctx_pass(0)
    wo_event(1, 3)
    z_pass("B", 0, 1)
    z_event("A", 0, 1)
    z_start("A", 1)
    z_start("A", 2)
    ctx_pass(1)
    y_event("B", 0, 1)
    ctx_pass(2)
    wo_event(0, 4)
    wo_event(1, 4)
    ctx_pass(3)
    for copy in res_loads:
        copy.wait()
    wo_d_wait()
    for k in range(4):
        ctx_end(k)
        project(k)
        if k == 0:
            z_event("A", -1, 1)
        if k == 1:
            y_event("B", 0, 2)
            y_event("B", -1, 1)
            y_event("B", 1, 1)
    z_event("B", 0, 2)
    y_start("B", 2)
    y_start("B", -2)
    z_event("A", 0, 2)
    z_event("A", 1, 1)
    z_event("A", 2, 1)
    stream_pass(0, 1)
    z_event("A", -1, 2)
    y_event("B", -1, 2)
    y_event("B", 1, 2)
    stream_pass(1, 1)
    stream_pass(0, 2)
    z_event("B", 0, 3)
    y_start("B", 3)
    y_start("B", -3)
    z_event("A", 0, 3)
    z_event("A", 1, 2)
    z_event("A", 2, 2)
    y_event("B", 2, 1)
    y_event("B", -2, 1)
    stream_pass(2, 1)
    stream_pass(1, 2)
    stream_end(0)
    norm_scale(0)
    ff_part(0, 0, 1, -1)
    z_event("A", -1, 3)
    z_event("B", 0, 4)
    y_start("B", 4)
    z_event("A", 1, 3)
    z_event("A", 2, 3)
    stream_pass(3, 1)
    stream_pass(2, 2)
    stream_end(1)
    norm_scale(1)
    ff_part(1, 0, 1, -1)
    y_event("B", 2, 2)
    y_event("B", -2, 2)
    ff_part(0, 2, -2)
    ff_part(1, 2, -2)
    y_event("B", 3, 1)
    y_event("B", -3, 1)
    y_event("B", 4, 1)
    stream_pass(3, 2)
    stream_end(2)
    norm_scale(2)
    ff_part(2, 0, 1, -1)
    ff_part(2, 2, -2)
    stream_end(3)
    norm_scale(3)
    for zz in range(Z):
        outs.append(local(stream.at[zz, mine, :], resid_out.at[:, 512 * zz : 512 * zz + 512]))
    ff_part(3, 0, 1, -1)
    ff_part(3, 2, -2)
    y_event("B", 3, 2)
    y_event("B", -3, 2)
    for k in range(4):
        ff_part(k, 3, -3)
    drain(len(sent))
    for dy in (0, -1, 1, 2):
        z_event("A", dy, 4)
    y_event("B", 4, 2)
    for k in range(4):
        ff_part(k, 4)
        activate(k)

    def final_wait():
        for copy in outs:
            copy.wait()
        for ahead in range(1, X):

            @pl.when((x + ahead) % X == y)
            def _(copy=gather[ahead]):
                copy.wait_send()

        @pl.when(collector)
        def _():
            for copy in spread:
                copy.wait_send()

        drain(len(sent))

    final_wait()
    assert state["send"] <= N_SEMS and len(recv_ids) <= N_SEMS


def body(queries, keys, values, spans, resid_in, out_weight, norm_gain, gate_weight, up_weight):
    anywhere = pl.BlockSpec(memory_space=pl.ANY)
    vmem = pl.BlockSpec(memory_space=pltpu.VMEM)
    smem = pl.BlockSpec(memory_space=pltpu.SMEM)
    resid_out, hidden = pl.pallas_call(
        kernel,
        out_shape=(jax.ShapeDtypeStruct((128, D), BF16), jax.ShapeDtypeStruct((FF, SEQ), BF16)),
        in_specs=[anywhere, anywhere, anywhere, smem, anywhere, vmem, vmem, vmem, vmem],
        out_specs=(anywhere, anywhere),
        scratch_shapes=[
            pltpu.VMEM((3, SEQ, 256), BF16),
            pltpu.VMEM((SEQ, 256), BF16),
            pltpu.VMEM((512, 2048), BF16),
            pltpu.VMEM((4, 128, 1024), BF16),
            pltpu.VMEM((Z, SEQ, 512), BF16),
            pltpu.VMEM((2048, 1024), BF16),
            pltpu.VMEM((Z, 2 * FF, 512), BF16),
            pltpu.VMEM((2 * FF, SEQ), F32),
            pltpu.VMEM((4, 1, 256), F32),
            pltpu.VMEM((FF, SEQ), BF16),
            pltpu.SemaphoreType.DMA((N_SEMS,)),
            pltpu.SemaphoreType.DMA((N_SEMS,)),
            pltpu.SemaphoreType.DMA((32,)),
        ],
        compiler_params=pltpu.CompilerParams(
            collective_id=0, has_side_effects=True, vmem_limit_bytes=56 * 1024 * 1024
        ),
    )(
        queries, keys, values, spans, resid_in.reshape(4, 2, 128, D), out_weight,
        norm_gain.reshape(D // 128, 128), gate_weight.T, up_weight.T,
    )
    return resid_out, hidden.T


def solution(mesh):
    return jax.shard_map(
        body,
        mesh=mesh,
        in_specs=(
            P(("dp", "ctx"), None),
            P(("dp", "ctx"), None),
            P(("dp", "ctx"), None),
            P("dp", None),
            P("dp", None),
            P("ctx", "dp"),
            P(),
            P("dp", "ctx"),
            P("dp", "ctx"),
        ),
        out_specs=(P(("dp", "ctx"), None), P("dp", "ctx")),
        check_vma=False,
    )
```

```python
import functools
import math

import jax
import jax.numpy as jnp
from jax import lax
from jax.experimental import pallas as pl
from jax.experimental.pallas import tpu as pltpu
from jax.sharding import PartitionSpec as P

MESH = pl.DeviceIdType.MESH
Z, Y, X = 8, 4, 4
HD = 128
SEQ, D, FF = 1024, 4096, 688
PART_ROWS = {"A": (0, 512), "B": (512, 2 * FF - 512)}
EXP2_SCALE = math.log2(math.e) / math.sqrt(HD)
F32, BF16 = jnp.float32, jnp.bfloat16
VMEM_BYTES = 56 * 1024 * 1024
N_SEND, N_RECV, N_LOCAL = 11, 73, 9


def mult(value, of):
    return pl.multiple_of(value, of)


def kernel(
    q_in, k_in, v_in, spans_in, resid, wo_in, gain_in, gate_hbm, up_hbm,
    resid_out, hidden,
    qkv, ctx_own, ctx_all, res, stream, wo, w, acc, scales, hid, gain, gate_in, up_in, spans,
    send_sem, recv_sem, local_sem,
):
    cx, dp = lax.axis_index("ctx"), lax.axis_index("dp")
    x, c = cx // 2, cx % 2
    z, y = dp // Y, dp % Y

    def dev(dz=0, dy=0, dx=0, dc=0):
        zz, yy = (z + dz + Z) % Z, (y + dy + Y) % Y
        xx, cc = (x + dx + X) % X, (c + dc) % 2
        return (zz * Y + yy, xx * 2 + cc)

    send_ids, recv_ids, local_ids = {}, {}, {}

    def remote(src, dst, target, kind, event):
        return pltpu.make_async_remote_copy(
            src_ref=src, dst_ref=dst, send_sem=send_sem.at[send_ids.setdefault(kind, len(send_ids))],
            recv_sem=recv_sem.at[recv_ids.setdefault(event, len(recv_ids))], device_id=target, device_id_type=MESH,
        )

    def send(src, dst, target, kind, event):
        remote(src, dst, target, kind, event).start()

    def recv(as_large, event):
        remote(as_large, as_large, dev(0, 0, 0, 1), "qkv", event).wait_recv()

    def sent(as_large, kind):
        remote(as_large, as_large, dev(0, 0, 0, 1), kind, "q").wait_send()

    def local(src, dst, kind):
        index = local_ids.setdefault(kind, len(local_ids))
        pltpu.make_async_copy(src, dst, local_sem.at[index]).start()

    def local_wait(as_large, kind):
        pltpu.make_async_copy(as_large, as_large, local_sem.at[local_ids[kind]]).wait()

    local(gate_hbm, gate_in, "gate")
    local(up_hbm, up_in, "up")
    local(gain_in.at[pl.ds(dp, 1), :], gain, "gain")
    local(spans_in, spans, "spans")

    barrier = pltpu.get_barrier_semaphore()
    peers = [(0, 0, dx, dc) for dx in range(X) for dc in range(2) if (dx, dc) != (0, 0)]
    peers += [(0, 1, 0, 0), (0, 2, 0, 0), (0, 3, 0, 0), (1, 0, 0, 0), (-1, 0, 0, 0)]
    for peer in peers:
        pl.semaphore_signal(barrier, inc=1, device_id=dev(*peer), device_id_type=MESH)
    pl.semaphore_wait(barrier, len(peers))

    def wo_block(zz, cc, unit=None):
        rows = pl.ds(mult(cc * 1024, 1024), 1024) if unit is None else pl.ds(mult(cc * 1024 + unit * 512, 512), 512)
        return wo.at[rows, pl.ds(mult((zz + Z) % Z * 128, 128), 128)]

    def wo_rows(xx):
        return wo.at[pl.ds(mult(c * 1024 + xx * 256, 256), 256), pl.ds(mult(z * 128, 128), 128)]

    ahead = (y - x + X) % X
    collector = ahead == 0

    @pl.when(jnp.logical_not(collector))
    def _():
        send(wo_in, wo_rows(x), dev(0, 0, ahead, 0), "wo_x", "wo_x")

    def pack_own():
        local_wait(gate_in, "gate")
        local_wait(up_in, "up")
        local_wait(gain, "gain")
        gain_row = gain[...]
        columns = pl.ds(mult(y * 128, 128), 128)
        w[z, :FF, columns] = (gate_in[...].astype(F32) * gain_row).astype(BF16)
        w[z, FF:, columns] = (up_in[...].astype(F32) * gain_row).astype(BF16)

    pack_own()

    def w_block(part, dz, dy, half=None):
        first, count = PART_ROWS[part]
        if half is not None:
            first, count = first + half * count // 2, count // 2
        return w.at[(z + dz + Z) % Z, first : first + count, pl.ds(mult((y + dy + Y) % Y * 128, 128), 128)]

    def w_like(part, z_blocks, y_blocks):
        first, count = PART_ROWS[part]
        return w.at[:z_blocks, first : first + count, : 128 * y_blocks]

    def z_send(part, dz, dy, d, hop, half=None):
        ref = w_block(part, dz, dy, half)
        send(ref, ref, dev(d, 0, 0, 0), (part, "z"), (part, "z", dy, hop))

    def y_send(part, dz, dy, d, hop, half=None):
        ref = w_block(part, dz, dy, half)
        send(ref, ref, dev(0, d, 0, 0), (part, "y"), (part, "y", dz, hop))

    def z_start(part, dy):
        for d in (1, -1):
            z_send(part, 0, dy, d, 1)

    def z_wait(part, dy, hop):
        recv(w_like(part, 2 if hop < 4 else 1, 1), (part, "z", dy, hop))

    def z_pass(part, dy, hop):
        for d in (1, -1):
            half = None if hop < 3 else (0 if d == 1 else 1)
            z_send(part, -d * hop, dy, d, hop + 1, half)

    def z_event(part, dy, hop):
        z_wait(part, dy, hop)
        if hop < 4:
            z_pass(part, dy, hop)

    def y_start(part, dz):
        for d in (1, -1):
            y_send(part, dz, 0, d, 1)

    def y_event(part, dz, hop):
        recv(w_like(part, 2 if hop < 2 else 1, 1), (part, "y", dz, hop))
        if hop == 1:
            for d in (1, -1):
                y_send(part, dz, -d, d, 2, 0 if d == 1 else 1)

    y_start("A", 0)
    z_start("B", 0)
    z_start("A", 0)

    mine = pl.ds(mult(cx * 128, 128), 128)
    shares = {"k": (1, k_in), "v": (2, v_in), "q": (0, q_in)}

    def share(name):
        which, source = shares[name]
        for dx, dc in [(2, 0), (2, 1), (1, 0), (1, 1), (3, 0), (3, 1), (0, 1)]:
            target = dev(0, 0, dx, dc)
            columns = pl.ds(mult(target[1] * 256, 256), 256)
            send(source.at[:, columns], qkv.at[which, mine], target, "qkv", name)
        local(source.at[:, pl.ds(mult(cx * 256, 256), 256)], qkv.at[which, mine], "qkv")

    share("k")

    @pl.when(collector)
    def _():
        recv(wo.at[:256, :384], "wo_x")
        own_part = pltpu.make_async_copy(wo_in, wo_rows(x), local_sem.at[local_ids.setdefault("wo", len(local_ids))])
        own_part.start()
        own_part.wait()
        for unit in range(2):
            for d in (1, -1):
                ref = wo_block(z, c, unit)
                send(ref, ref, dev(0, d, 0, 0), "wo_y", ("wo_y", unit))

    def wo_y_wait(unit):
        @pl.when(jnp.logical_not(collector))
        def _():
            recv(wo_block(z, c, unit), ("wo_y", unit))

        d = 1 if unit == 0 else -1

        @pl.when(ahead == d % Y)
        def _():
            ref = wo_block(z, c, unit)
            send(ref, ref, dev(0, d, 0, 0), "wo_y", ("wo_y", unit))

    def wo_across(dz, unit):
        ref = wo_block(z + dz, c, unit)
        send(ref, ref, dev(0, 0, 0, 1), "wo_d", "wo_d")

    def wo_start(unit):
        ref = wo_block(z, c, unit)
        for d in (1, -1):
            send(ref, ref, dev(d, 0, 0, 0), "wo_z", ("wo_z", unit, 1))
        wo_across(0, unit)

    def wo_event(unit, hop):
        recv(wo_block(0, 0, 0) if hop == 4 else wo.at[:512, :256], ("wo_z", unit, hop))
        for d in (1, -1):
            if hop == 4 and unit != (0 if d == 1 else 1):
                continue
            ref = wo_block(z - d * hop, c, unit)
            if hop < 3 or (hop == 3 and unit == (0 if d == 1 else 1)):
                send(ref, ref, dev(d, 0, 0, 0), "wo_z", ("wo_z", unit, hop + 1))
            wo_across(4 if hop == 4 else -d * hop, unit)

    def wo_d_wait():
        recv(wo.at[:1024, :], "wo_d")

    def qkv_wait():
        local_wait(qkv.at[:, :128, :], "qkv")
        for name in shares:
            recv(qkv.at[0, :896], name)

    local_wait(spans, "spans")
    prefix_end, middle_end = spans[0, 0], spans[0, 1]

    def ranks(pos):
        late = prefix_end + (SEQ - middle_end) + (pos - prefix_end)
        return jnp.where(pos < prefix_end, pos, jnp.where(pos >= middle_end, prefix_end + pos - middle_end, late))

    key_rank = ranks(lax.broadcasted_iota(jnp.int32, (1, SEQ), 1))

    def ctx_spot(k, cc, xx, half=None):
        rows = pl.ds(128 * k, 128) if half is None else pl.ds(128 * k + 64 * half, 64)
        return ctx_all.at[rows, pl.ds(mult(cc * 1024 + xx * 256, 256), 256)]

    def attend(k, rel):
        row = mult((2 * k + (c + rel) % 2) * 128, 128)
        rows = pl.ds(row, 128)
        query_rank = ranks(row + lax.broadcasted_iota(jnp.int32, (128, 1), 0))
        allowed = query_rank >= key_rank
        for head in range(2):
            cols = slice(head * HD, head * HD + HD)
            scores = lax.dot_general(
                qkv[0, rows, cols], qkv[1, :, cols], (((1,), (1,)), ((), ())), preferred_element_type=F32
            )
            scores = jnp.where(allowed, scores, -jnp.inf)
            peak = jnp.max(scores, axis=1, keepdims=True)
            expo = jnp.exp2((scores - peak) * EXP2_SCALE)
            total = jnp.sum(expo, axis=1, keepdims=True)
            mixed = jnp.dot(expo.astype(BF16), qkv[2, :, cols], preferred_element_type=F32)
            mixed = (mixed / total).astype(BF16)
            ctx_own[rows, cols] = mixed
            if rel == 0:
                ctx_all[128 * k : 128 * k + 128, pl.ds(mult(c * 1024 + x * 256 + head * HD, 128), HD)] = mixed
        for d in (1, -1):
            send(ctx_own.at[rows], ctx_spot(k, c, x), dev(0, 0, d, rel), "ctx", ("ctx", k, 1))
        if rel == 1:
            send(ctx_own.at[rows], ctx_spot(k, c, x), dev(0, 0, 0, 1), "ctx", ("ctx", k, 2))

    def ctx_pass(k):
        recv(ctx_all.at[:128, :1024], ("ctx", k, 1))
        for rel in range(2):
            for d in (1, -1):
                ref = ctx_spot(k, (c + rel) % 2, (x - d + X) % X, 0 if d == 1 else 1)
                send(ref, ref, dev(0, 0, d, 0), "ctx", ("ctx", k, 2))

    def ctx_end(k):
        recv(ctx_all.at[:128, :768], ("ctx", k, 2))

    for zz in range(Z):
        columns = pl.ds(mult(zz * 512 + x * 128, 128), 128)
        local(resid.at[:, c, :, columns], res.at[:, :, 128 * zz : 128 * zz + 128], "res")

    def stream_spot(k, cc, xx, half=None):
        row = (2 * k + cc) * 128
        rows = pl.ds(mult(row, 128), 128) if half is None else pl.ds(mult(row + half * 64, 64), 64)
        return stream.at[:, rows, pl.ds(mult(xx * 128, 128), 128)]

    def project(k):
        rows = pl.ds(mult((2 * k + c) * 128, 128), 128)
        columns = pl.ds(mult(x * 128, 128), 128)
        for block in range(4):
            part = jnp.dot(
                ctx_all[128 * k : 128 * k + 128, :], wo[:, 256 * block : 256 * block + 256], preferred_element_type=F32
            )
            part = part + res[k, :, 256 * block : 256 * block + 256].astype(F32)
            stream[2 * block, rows, columns] = part[:, :128].astype(BF16)
            stream[2 * block + 1, rows, columns] = part[:, 128:].astype(BF16)
        ref = stream_spot(k, c, x)
        for d in (1, -1):
            send(ref, ref, dev(0, 0, d, 0), "stream", ("stream", k, 1))
        send(ref, ref, dev(0, 0, 0, 1), "stream", ("across", k))

    def stream_pass(k, hop):
        recv(stream.at[:, : 256 // hop, :128], ("stream", k, hop))
        for d in (1, -1):
            half = 0 if d == 1 else 1
            if hop == 1:
                ref = stream_spot(k, c, (x - d + X) % X, half)
                send(ref, ref, dev(0, 0, d, 0), "stream", ("stream", k, 2))
            ref = stream_spot(k, c, (x - d * hop + X) % X, None if hop == 1 else half)
            send(ref, ref, dev(0, 0, 0, 1), "stream", ("across", k))

    def stream_end(k):
        recv(stream.at[:, :128, :], ("across", k))

    def norm_scale(k):
        rows = pl.ds(256 * k, 256)

        def add_squares(i, total):
            piece = stream[i, rows, :].astype(F32)
            piece = piece * piece
            return total + (piece[:, :128] + piece[:, 128:256]) + (piece[:, 256:384] + piece[:, 384:])

        squares = lax.fori_loop(0, Z, add_squares, jnp.zeros((256, 128), F32))
        total = jnp.sum(squares.T, axis=0, keepdims=True)
        scales[k] = lax.rsqrt(total * (1.0 / D) + 1e-5)

    def ff_part(k, *dzs):
        rows = slice(256 * k, 256 * k + 256)

        def one(half, _):
            at = pl.ds(mult(half * FF, 16), FF)
            total = None
            for dz in dzs:
                zz = (z + dz + Z) % Z
                part = lax.dot_general(
                    w[zz, at, :], stream[zz, rows, :], (((1,), (1,)), ((), ())), preferred_element_type=F32
                )
                total = part if total is None else total + part
            acc[at, rows] = total if 0 in dzs else acc[at, rows] + total
            return 0

        lax.fori_loop(0, 2, one, 0)

    def activate(k):
        rows = slice(256 * k, 256 * k + 256)
        scale = scales[k]
        for first in range(0, FF, 128):
            count = min(128, FF - first)
            gate = acc[first : first + count, rows] * scale
            up = acc[FF + first : FF + first + count, rows] * scale
            hid[first : first + count, rows] = (gate / (1.0 + jnp.exp(-gate)) * up).astype(BF16)
        local(hid.at[:, rows], hidden.at[:, rows], "hidden")

    y_event("A", 0, 1)
    share("v")
    share("q")
    z_start("A", -1)
    z_event("B", 0, 1)
    for unit in range(2):
        wo_y_wait(unit)
        wo_start(unit)
    y_start("B", 0)
    y_start("B", 1)
    y_start("B", -1)
    wo_event(0, 1)
    wo_event(1, 1)
    qkv_wait()
    attend(0, 1)
    attend(0, 0)
    wo_event(0, 2)
    attend(1, 1)
    attend(1, 0)
    wo_event(1, 2)
    z_wait("B", 0, 2)
    y_start("B", 2)
    y_start("B", -2)
    attend(2, 1)
    attend(2, 0)
    y_event("A", 0, 2)
    attend(3, 1)
    attend(3, 0)
    wo_event(0, 3)
    z_pass("B", 0, 2)
    ctx_pass(0)
    wo_event(1, 3)
    z_event("A", 0, 1)
    z_start("A", 1)
    ctx_pass(1)
    z_start("A", 2)
    y_event("B", 0, 1)
    wo_event(0, 4)
    wo_event(1, 4)
    ctx_pass(2)
    z_event("A", -1, 1)
    ctx_pass(3)
    local_wait(res, "res")
    wo_d_wait()
    ctx_end(0)
    project(0)
    y_event("B", -1, 1)
    y_event("B", 1, 1)
    ctx_end(1)
    project(1)
    z_event("B", 0, 3)
    y_start("B", 3)
    y_start("B", -3)
    y_event("B", 0, 2)
    stream_pass(0, 1)
    ctx_end(2)
    project(2)
    z_event("A", 0, 2)
    z_event("A", 1, 1)
    y_event("B", 2, 1)
    y_event("B", -2, 1)
    stream_pass(1, 1)
    ctx_end(3)
    project(3)
    z_event("A", 2, 1)
    z_event("A", -1, 2)
    z_event("B", 0, 4)
    y_start("B", 4)
    stream_pass(0, 2)
    y_event("B", -1, 2)
    y_event("B", 1, 2)
    stream_end(0)
    norm_scale(0)
    z_event("A", 0, 3)
    z_event("A", 1, 2)
    y_event("B", 3, 1)
    y_event("B", -3, 1)
    stream_pass(2, 1)
    ff_part(0, 0, 1, -1)
    z_event("A", 2, 2)
    z_event("A", -1, 3)
    stream_pass(1, 2)
    stream_end(1)
    norm_scale(1)
    ff_part(1, 0, 1, -1)
    y_event("B", 4, 1)
    stream_pass(3, 1)
    z_event("A", 1, 3)
    z_event("A", 2, 3)
    y_event("B", 2, 2)
    y_event("B", -2, 2)
    ff_part(0, 2, -2)
    stream_pass(2, 2)
    ff_part(1, 2, -2)
    stream_end(2)
    norm_scale(2)
    ff_part(2, 0, 1, -1)
    stream_pass(3, 2)
    ff_part(2, 2, -2)
    stream_end(3)
    norm_scale(3)
    for zz in range(Z):
        local(stream.at[zz, mine, :], resid_out.at[:, 512 * zz : 512 * zz + 512], "resid_out")
    ff_part(3, 0, 1, -1)
    ff_part(3, 2, -2)

    def early_sent():
        @pl.when(jnp.logical_not(collector))
        def _():
            sent(wo_in, "wo_x")

        @pl.when(collector)
        def _():
            sent(wo.at[:512, :512], "wo_y")

        @pl.when(ahead % 2 == 1)
        def _():
            sent(wo_block(0, 0, 0), "wo_y")

        sent(wo.at[:1024, :896], "wo_z")
        sent(wo.at[:1024, :], "wo_d")
        sent(qkv.at[:, :896], "qkv")
        sent(ctx_all.at[:448, :], "ctx")
        sent(stream.at[:, :896, :], "stream")
        sent(w_like("A", 3, 1), ("A", "y"))

    early_sent()
    y_event("B", 3, 2)
    y_event("B", -3, 2)
    for k in range(4):
        ff_part(k, 3, -3)
    for dy in (0, -1, 1, 2):
        z_event("A", dy, 4)
    y_event("B", 4, 2)
    for k in range(4):
        ff_part(k, 4)
        activate(k)
    sent(w_like("A", 7, 4), ("A", "z"))
    sent(w_like("B", 7, 1), ("B", "z"))
    sent(w_like("B", 6, 4), ("B", "y"))
    local_wait(stream.at[:4, :256, :], "resid_out")
    local_wait(hid, "hidden")
    assert (len(send_ids), len(recv_ids), len(local_ids)) == (N_SEND, N_RECV, N_LOCAL), (send_ids, recv_ids, local_ids)


def body(queries, keys, values, spans, resid_in, out_weight, norm_gain, gate_weight, up_weight):
    anywhere = pl.BlockSpec(memory_space=pl.ANY)
    resid_out, hidden = pl.pallas_call(
        kernel,
        out_shape=(jax.ShapeDtypeStruct((128, D), BF16), jax.ShapeDtypeStruct((FF, SEQ), BF16)),
        in_specs=[pl.BlockSpec(memory_space=pltpu.HBM)] * 9,
        out_specs=(anywhere, anywhere),
        scratch_shapes=[
            pltpu.VMEM((3, SEQ, 256), BF16),
            pltpu.VMEM((SEQ, 256), BF16),
            pltpu.VMEM((512, 2048), BF16),
            pltpu.VMEM((4, 128, 1024), BF16),
            pltpu.VMEM((Z, SEQ, 512), BF16),
            pltpu.VMEM((2048, 1024), BF16),
            pltpu.VMEM((Z, 2 * FF, 512), BF16),
            pltpu.VMEM((2 * FF, SEQ), F32),
            pltpu.VMEM((4, 1, 256), F32),
            pltpu.VMEM((FF, SEQ), BF16),
            pltpu.VMEM((1, 128), F32),
            pltpu.VMEM((FF, 128), BF16),
            pltpu.VMEM((FF, 128), BF16),
            pltpu.SMEM((1, 2), jnp.int32),
            pltpu.SemaphoreType.DMA((N_SEND,)),
            pltpu.SemaphoreType.DMA((N_RECV,)),
            pltpu.SemaphoreType.DMA((N_LOCAL,)),
        ],
        compiler_params=pltpu.CompilerParams(
            collective_id=0, has_side_effects=True, vmem_limit_bytes=VMEM_BYTES
        ),
    )(
        queries, keys, values, spans, resid_in.reshape(4, 2, 128, D), out_weight,
        norm_gain.reshape(D // 128, 128), gate_weight.T, up_weight.T,
    )
    return resid_out, hidden.T


def solution(mesh):
    return jax.shard_map(
        body,
        mesh=mesh,
        in_specs=(
            P(("dp", "ctx"), None),
            P(("dp", "ctx"), None),
            P(("dp", "ctx"), None),
            P("dp", None),
            P("dp", None),
            P("ctx", "dp"),
            P(),
            P("dp", "ctx"),
            P("dp", "ctx"),
        ),
        out_specs=(P(("dp", "ctx"), None), P("dp", "ctx")),
        check_vma=False,
    )
```

```python
import functools
import math

import jax
import jax.numpy as jnp
from jax import lax
from jax.experimental import pallas as pl
from jax.experimental.pallas import tpu as pltpu
from jax.sharding import PartitionSpec as P

MESH = pl.DeviceIdType.MESH
Z, Y, X = 8, 4, 4
HD = 128
SEQ, D, FF = 1024, 4096, 688
PART_ROWS = {"A": (0, 448), "B": (448, 2 * FF - 448)}
EXP2_SCALE = math.log2(math.e) / math.sqrt(HD)
F32, BF16 = jnp.float32, jnp.bfloat16
VMEM_BYTES = 56 * 1024 * 1024
N_SEND, N_RECV, N_LOCAL = 11, 73, 9


def mult(value, of):
    return pl.multiple_of(value, of)


def kernel(
    q_in, k_in, v_in, spans_in, resid, wo_in, gain_in, gate_hbm, up_hbm,
    resid_out, hidden,
    qkv, ctx_own, ctx_all, res, stream, wo, w, acc, scales, hid, gain, gate_in, up_in, spans,
    send_sem, recv_sem, local_sem,
):
    cx, dp = lax.axis_index("ctx"), lax.axis_index("dp")
    x, c = cx // 2, cx % 2
    z, y = dp // Y, dp % Y

    def dev(dz=0, dy=0, dx=0, dc=0):
        zz, yy = (z + dz + Z) % Z, (y + dy + Y) % Y
        xx, cc = (x + dx + X) % X, (c + dc) % 2
        return (zz * Y + yy, xx * 2 + cc)

    send_ids, recv_ids, local_ids = {}, {}, {}

    def remote(src, dst, target, kind, event):
        return pltpu.make_async_remote_copy(
            src_ref=src, dst_ref=dst, send_sem=send_sem.at[send_ids.setdefault(kind, len(send_ids))],
            recv_sem=recv_sem.at[recv_ids.setdefault(event, len(recv_ids))], device_id=target, device_id_type=MESH,
        )

    def send(src, dst, target, kind, event):
        remote(src, dst, target, kind, event).start()

    def recv(as_large, event):
        remote(as_large, as_large, dev(0, 0, 0, 1), "qkv", event).wait_recv()

    def sent(as_large, kind):
        remote(as_large, as_large, dev(0, 0, 0, 1), kind, "q").wait_send()

    def local(src, dst, kind):
        index = local_ids.setdefault(kind, len(local_ids))
        pltpu.make_async_copy(src, dst, local_sem.at[index]).start()

    def local_wait(as_large, kind):
        pltpu.make_async_copy(as_large, as_large, local_sem.at[local_ids[kind]]).wait()

    local(gate_hbm, gate_in, "gate")
    local(up_hbm, up_in, "up")
    local(gain_in.at[pl.ds(dp, 1), :], gain, "gain")
    local(spans_in, spans, "spans")

    barrier = pltpu.get_barrier_semaphore()
    peers = [(0, 0, dx, dc) for dx in range(X) for dc in range(2) if (dx, dc) != (0, 0)]
    peers += [(0, 1, 0, 0), (0, 2, 0, 0), (0, 3, 0, 0), (1, 0, 0, 0), (-1, 0, 0, 0)]
    for peer in peers:
        pl.semaphore_signal(barrier, inc=1, device_id=dev(*peer), device_id_type=MESH)

    def wo_block(zz, cc, unit=None):
        rows = pl.ds(mult(cc * 1024, 1024), 1024) if unit is None else pl.ds(mult(cc * 1024 + unit * 512, 512), 512)
        return wo.at[rows, pl.ds(mult((zz + Z) % Z * 128, 128), 128)]

    def wo_rows(xx):
        return wo.at[pl.ds(mult(c * 1024 + xx * 256, 256), 256), pl.ds(mult(z * 128, 128), 128)]

    ahead = (y - x + X) % X
    collector = ahead == 0

    def pack_own():
        local_wait(gate_in, "gate")
        local_wait(up_in, "up")
        local_wait(gain, "gain")
        gain_row = gain[...]
        columns = pl.ds(mult(y * 128, 128), 128)
        w[z, :FF, columns] = (gate_in[...].astype(F32) * gain_row).astype(BF16)
        w[z, FF:, columns] = (up_in[...].astype(F32) * gain_row).astype(BF16)

    pack_own()
    pl.semaphore_wait(barrier, len(peers))

    @pl.when(jnp.logical_not(collector))
    def _():
        for piece in range(4):
            rows = pl.ds(mult(c * 1024 + x * 256 + piece * 64, 64), 64)
            target = wo.at[rows, pl.ds(mult(z * 128, 128), 128)]
            send(wo_in.at[64 * piece : 64 * piece + 64, :], target, dev(0, 0, ahead, 0), "wo_x", "wo_x")

    def w_block(part, dz, dy, half=None):
        first, count = PART_ROWS[part]
        if half is not None:
            first, count = first + half * count // 2, count // 2
        return w.at[(z + dz + Z) % Z, first : first + count, pl.ds(mult((y + dy + Y) % Y * 128, 128), 128)]

    def w_like(part, z_blocks, y_blocks):
        first, count = PART_ROWS[part]
        return w.at[:z_blocks, first : first + count, : 128 * y_blocks]

    def z_send(part, dz, dy, d, hop, half=None):
        ref = w_block(part, dz, dy, half)
        send(ref, ref, dev(d, 0, 0, 0), (part, "z"), (part, "z", dy, hop))

    def y_send(part, dz, dy, d, hop, half=None):
        ref = w_block(part, dz, dy, half)
        send(ref, ref, dev(0, d, 0, 0), (part, "y"), (part, "y", dz, hop))

    def z_start(part, dy):
        for d in (1, -1):
            z_send(part, 0, dy, d, 1)

    def z_wait(part, dy, hop):
        recv(w_like(part, 2 if hop < 4 else 1, 1), (part, "z", dy, hop))

    def z_pass(part, dy, hop):
        for d in (1, -1):
            half = None if hop < 3 else (0 if d == 1 else 1)
            z_send(part, -d * hop, dy, d, hop + 1, half)

    def z_event(part, dy, hop):
        z_wait(part, dy, hop)
        if hop < 4:
            z_pass(part, dy, hop)

    def y_start(part, dz):
        for d in (1, -1):
            y_send(part, dz, 0, d, 1)

    def y_event(part, dz, hop):
        recv(w_like(part, 2 if hop < 2 else 1, 1), (part, "y", dz, hop))
        if hop == 1:
            for d in (1, -1):
                y_send(part, dz, -d, d, 2, 0 if d == 1 else 1)

    y_start("A", 0)
    z_start("B", 0)
    z_start("A", 0)

    @pl.when(jnp.logical_not(collector))
    def _():
        y_start("B", 0)

    mine = pl.ds(mult(cx * 128, 128), 128)
    shares = {"k": (1, k_in), "v": (2, v_in), "q": (0, q_in)}

    def share(name):
        which, source = shares[name]
        for dx, dc in [(2, 0), (2, 1), (1, 0), (1, 1), (3, 0), (3, 1), (0, 1)]:
            target = dev(0, 0, dx, dc)
            columns = pl.ds(mult(target[1] * 256, 256), 256)
            send(source.at[:, columns], qkv.at[which, mine], target, "qkv", name)
        local(source.at[:, pl.ds(mult(cx * 256, 256), 256)], qkv.at[which, mine], "qkv")

    share("k")

    def wo_along_y(unit, d):
        ref = wo_block(z, c, unit)
        send(ref, ref, dev(0, d, 0, 0), "wo_y", ("wo_y", unit))

    @pl.when(collector)
    def _():
        recv(wo.at[:256, :384], "wo_x")
        own_part = pltpu.make_async_copy(wo_in, wo_rows(x), local_sem.at[local_ids.setdefault("wo", len(local_ids))])
        own_part.start()
        own_part.wait()
        wo_along_y(0, 1)
        wo_along_y(1, -1)

    def wo_y_wait(unit):
        @pl.when(jnp.logical_not(collector))
        def _():
            recv(wo_block(z, c, unit), ("wo_y", unit))

        d = 1 if unit == 0 else -1

        @pl.when(ahead == d % Y)
        def _():
            wo_along_y(unit, d)

    def wo_across(dz, unit):
        ref = wo_block(z + dz, c, unit)
        send(ref, ref, dev(0, 0, 0, 1), "wo_d", "wo_d")

    def wo_start(unit):
        ref = wo_block(z, c, unit)
        for d in (1, -1):
            send(ref, ref, dev(d, 0, 0, 0), "wo_z", ("wo_z", unit, 1))
        wo_across(0, unit)

    def wo_event(unit, hop):
        recv(wo_block(0, 0, 0) if hop == 4 else wo.at[:512, :256], ("wo_z", unit, hop))
        for d in (1, -1):
            if hop == 4 and unit != (0 if d == 1 else 1):
                continue
            ref = wo_block(z - d * hop, c, unit)
            if hop < 3 or (hop == 3 and unit == (0 if d == 1 else 1)):
                send(ref, ref, dev(d, 0, 0, 0), "wo_z", ("wo_z", unit, hop + 1))
            wo_across(4 if hop == 4 else -d * hop, unit)

    def wo_d_wait():
        recv(wo.at[:1024, :], "wo_d")

    def qkv_wait():
        local_wait(qkv.at[:, :128, :], "qkv")
        for name in shares:
            recv(qkv.at[0, :896], name)

    local_wait(spans, "spans")
    prefix_end, middle_end = spans[0, 0], spans[0, 1]

    def ranks(pos):
        late = prefix_end + (SEQ - middle_end) + (pos - prefix_end)
        return jnp.where(pos < prefix_end, pos, jnp.where(pos >= middle_end, prefix_end + pos - middle_end, late))

    key_rank = ranks(lax.broadcasted_iota(jnp.int32, (1, SEQ), 1))

    def ctx_spot(k, cc, xx, half=None):
        rows = pl.ds(128 * k, 128) if half is None else pl.ds(128 * k + 64 * half, 64)
        return ctx_all.at[rows, pl.ds(mult(cc * 1024 + xx * 256, 256), 256)]

    def attend(k, rel):
        row = mult((2 * k + (c + rel) % 2) * 128, 128)
        rows = pl.ds(row, 128)
        query_rank = ranks(row + lax.broadcasted_iota(jnp.int32, (128, 1), 0))
        allowed = query_rank >= key_rank
        for head in range(2):
            cols = slice(head * HD, head * HD + HD)
            scores = lax.dot_general(
                qkv[0, rows, cols], qkv[1, :, cols], (((1,), (1,)), ((), ())), preferred_element_type=F32
            )
            scores = jnp.where(allowed, scores, -jnp.inf)
            peak = jnp.max(scores, axis=1, keepdims=True)
            expo = jnp.exp2((scores - peak) * EXP2_SCALE)
            total = jnp.sum(expo, axis=1, keepdims=True)
            mixed = jnp.dot(expo.astype(BF16), qkv[2, :, cols], preferred_element_type=F32)
            mixed = (mixed / total).astype(BF16)
            ctx_own[rows, cols] = mixed
            if rel == 0:
                ctx_all[128 * k : 128 * k + 128, pl.ds(mult(c * 1024 + x * 256 + head * HD, 128), HD)] = mixed
        for d in (1, -1):
            send(ctx_own.at[rows], ctx_spot(k, c, x), dev(0, 0, d, rel), "ctx", ("ctx", k, 1))
        if rel == 1:
            send(ctx_own.at[rows], ctx_spot(k, c, x), dev(0, 0, 0, 1), "ctx", ("ctx", k, 2))

    def ctx_pass(k):
        recv(ctx_all.at[:128, :1024], ("ctx", k, 1))
        for rel in range(2):
            for d in (1, -1):
                ref = ctx_spot(k, (c + rel) % 2, (x - d + X) % X, 0 if d == 1 else 1)
                send(ref, ref, dev(0, 0, d, 0), "ctx", ("ctx", k, 2))

    def ctx_end(k):
        recv(ctx_all.at[:128, :768], ("ctx", k, 2))

    for zz in range(Z):
        columns = pl.ds(mult(zz * 512 + x * 128, 128), 128)
        local(resid.at[:, c, :, columns], res.at[:, :, 128 * zz : 128 * zz + 128], "res")

    def stream_spot(k, cc, xx, half=None):
        row = (2 * k + cc) * 128
        rows = pl.ds(mult(row, 128), 128) if half is None else pl.ds(mult(row + half * 64, 64), 64)
        return stream.at[:, rows, pl.ds(mult(xx * 128, 128), 128)]

    def project(k):
        rows = pl.ds(mult((2 * k + c) * 128, 128), 128)
        columns = pl.ds(mult(x * 128, 128), 128)
        for block in range(4):
            part = jnp.dot(
                ctx_all[128 * k : 128 * k + 128, :], wo[:, 256 * block : 256 * block + 256], preferred_element_type=F32
            )
            part = part + res[k, :, 256 * block : 256 * block + 256].astype(F32)
            stream[2 * block, rows, columns] = part[:, :128].astype(BF16)
            stream[2 * block + 1, rows, columns] = part[:, 128:].astype(BF16)
        ref = stream_spot(k, c, x)
        for d in (1, -1):
            send(ref, ref, dev(0, 0, d, 0), "stream", ("stream", k, 1))
        send(ref, ref, dev(0, 0, 0, 1), "stream", ("across", k))

    def stream_pass(k, hop):
        recv(stream.at[:, : 256 // hop, :128], ("stream", k, hop))
        for d in (1, -1):
            half = 0 if d == 1 else 1
            if hop == 1:
                ref = stream_spot(k, c, (x - d + X) % X, half)
                send(ref, ref, dev(0, 0, d, 0), "stream", ("stream", k, 2))
            ref = stream_spot(k, c, (x - d * hop + X) % X, None if hop == 1 else half)
            send(ref, ref, dev(0, 0, 0, 1), "stream", ("across", k))

    def stream_end(k):
        recv(stream.at[:, :128, :], ("across", k))

    def norm_scale(k):
        rows = pl.ds(256 * k, 256)

        def add_squares(i, total):
            piece = stream[i, rows, :].astype(F32)
            piece = piece * piece
            return total + (piece[:, :128] + piece[:, 128:256]) + (piece[:, 256:384] + piece[:, 384:])

        squares = lax.fori_loop(0, Z, add_squares, jnp.zeros((256, 128), F32))
        total = jnp.sum(squares.T, axis=0, keepdims=True)
        scales[k] = lax.rsqrt(total * (1.0 / D) + 1e-5)

    def ff_part(k, *dzs):
        rows = slice(256 * k, 256 * k + 256)

        def one(half, _):
            at = pl.ds(mult(half * FF, 16), FF)
            total = None
            for dz in dzs:
                zz = (z + dz + Z) % Z
                part = lax.dot_general(
                    w[zz, at, :], stream[zz, rows, :], (((1,), (1,)), ((), ())), preferred_element_type=F32
                )
                total = part if total is None else total + part
            acc[at, rows] = total if 0 in dzs else acc[at, rows] + total
            return 0

        lax.fori_loop(0, 2, one, 0)

    def activate(k):
        rows = slice(256 * k, 256 * k + 256)
        scale = scales[k]
        for first in range(0, FF, 128):
            count = min(128, FF - first)
            gate = acc[first : first + count, rows] * scale
            up = acc[FF + first : FF + first + count, rows] * scale
            hid[first : first + count, rows] = (gate / (1.0 + jnp.exp(-gate)) * up).astype(BF16)
            if first in (256, 640):
                done = slice(0, 384) if first == 256 else slice(384, FF)
                local(hid.at[done, rows], hidden.at[done, rows], "hidden")

    y_event("A", 0, 1)
    share("v")
    share("q")

    def fill_z():
        z_start("A", -1)
        z_pass("B", 0, 1)

    z_wait("B", 0, 1)

    @pl.when(collector)
    def _():
        wo_along_y(1, 1)
        wo_along_y(0, -1)

    @pl.when(jnp.logical_not(collector))
    def _():
        fill_z()

    def next_y():
        y_start("B", 1)
        y_start("B", -1)

    @pl.when(ahead == 2)
    def _():
        next_y()

    def wo_units(*units):
        for unit in units:
            wo_y_wait(unit)
            wo_start(unit)

    @pl.when(ahead == 3)
    def _():
        wo_units(1, 0)

    @pl.when(ahead != 3)
    def _():
        wo_units(0, 1)

    @pl.when(collector)
    def _():
        y_start("B", 0)
        wo_event(0, 1)
        wo_event(1, 1)
        fill_z()

    @pl.when(ahead != 2)
    def _():
        next_y()

    qkv_wait()
    attend(0, 1)
    attend(0, 0)

    @pl.when(jnp.logical_not(collector))
    def _():
        wo_event(0, 1)

    attend(1, 1)
    attend(1, 0)

    @pl.when(jnp.logical_not(collector))
    def _():
        wo_event(1, 1)

    y_event("B", 0, 1)
    attend(2, 1)
    attend(2, 0)
    wo_event(0, 2)
    attend(3, 1)
    attend(3, 0)
    wo_event(1, 2)
    z_wait("B", 0, 2)
    y_start("B", 2)
    y_start("B", -2)
    ctx_pass(0)
    wo_event(0, 3)
    ctx_pass(1)
    y_event("A", 0, 2)
    wo_event(1, 3)
    z_pass("B", 0, 2)
    ctx_pass(2)
    y_event("B", -1, 1)
    y_event("B", 1, 1)
    wo_event(0, 4)
    wo_event(1, 4)
    z_event("A", 0, 1)
    z_start("A", 1)
    z_start("A", 2)
    ctx_pass(3)
    local_wait(res, "res")
    wo_d_wait()
    ctx_end(0)
    project(0)
    z_event("A", -1, 1)
    ctx_end(1)
    project(1)
    z_event("B", 0, 3)
    y_start("B", 3)
    y_start("B", -3)
    stream_pass(0, 1)
    ctx_end(2)
    project(2)
    y_event("B", 2, 1)
    y_event("B", -2, 1)
    z_event("A", 0, 2)
    z_event("A", 1, 1)
    z_event("A", 2, 1)
    z_event("A", -1, 2)
    stream_pass(1, 1)
    ctx_end(3)
    project(3)
    z_event("B", 0, 4)
    y_start("B", 4)
    stream_pass(0, 2)
    stream_end(0)
    norm_scale(0)
    y_event("B", 0, 2)
    y_event("B", -1, 2)
    y_event("B", 1, 2)
    ff_part(0, 0, 1, -1)
    stream_pass(2, 1)
    y_event("B", 3, 1)
    y_event("B", -3, 1)
    stream_pass(1, 2)
    z_event("A", 0, 3)
    z_event("A", 1, 2)
    z_event("A", 2, 2)
    z_event("A", -1, 3)
    stream_end(1)
    norm_scale(1)
    ff_part(1, 0, 1, -1)
    stream_pass(3, 1)
    y_event("B", 4, 1)
    y_event("B", 2, 2)
    y_event("B", -2, 2)
    ff_part(0, 2, -2)
    z_event("A", 1, 3)
    ff_part(1, 2, -2)
    stream_pass(2, 2)
    z_event("A", 2, 3)
    y_event("B", 3, 2)
    y_event("B", -3, 2)
    ff_part(0, 3, -3)
    stream_pass(3, 2)
    ff_part(1, 3, -3)
    stream_end(2)
    norm_scale(2)
    ff_part(2, 0, 1, -1, 2, -2, 3, -3)
    stream_end(3)
    for zz in range(Z):
        local(stream.at[zz, mine, :], resid_out.at[:, 512 * zz : 512 * zz + 512], "resid_out")
    norm_scale(3)

    def early_sent():
        @pl.when(jnp.logical_not(collector))
        def _():
            sent(wo_in, "wo_x")

        @pl.when(collector)
        def _():
            sent(wo.at[:512, :512], "wo_y")

        @pl.when(ahead % 2 == 1)
        def _():
            sent(wo_block(0, 0, 0), "wo_y")

        sent(wo.at[:1024, :896], "wo_z")
        sent(wo.at[:1024, :], "wo_d")
        sent(qkv.at[:, :896], "qkv")
        sent(ctx_all.at[:448, :], "ctx")
        sent(stream.at[:, :896, :], "stream")
        sent(w_like("A", 3, 1), ("A", "y"))

    early_sent()
    for dy in (0, -1, 1, 2):
        z_event("A", dy, 4)
    y_event("B", 4, 2)
    for k in range(3):
        ff_part(k, 4)
        activate(k)
    ff_part(3, 0, 1, -1, 2, -2, 3, -3, 4)
    activate(3)
    sent(w_like("A", 7, 4), ("A", "z"))
    sent(w_like("B", 7, 1), ("B", "z"))
    sent(w_like("B", 6, 4), ("B", "y"))
    local_wait(stream.at[:4, :256, :], "resid_out")
    local_wait(hid, "hidden")
    assert (len(send_ids), len(recv_ids), len(local_ids)) == (N_SEND, N_RECV, N_LOCAL), (send_ids, recv_ids, local_ids)


def body(queries, keys, values, spans, resid_in, out_weight, norm_gain, gate_weight, up_weight):
    anywhere = pl.BlockSpec(memory_space=pl.ANY)
    resid_out, hidden = pl.pallas_call(
        kernel,
        out_shape=(jax.ShapeDtypeStruct((128, D), BF16), jax.ShapeDtypeStruct((FF, SEQ), BF16)),
        in_specs=[pl.BlockSpec(memory_space=pltpu.HBM)] * 9,
        out_specs=(anywhere, anywhere),
        scratch_shapes=[
            pltpu.VMEM((3, SEQ, 256), BF16),
            pltpu.VMEM((SEQ, 256), BF16),
            pltpu.VMEM((512, 2048), BF16),
            pltpu.VMEM((4, 128, 1024), BF16),
            pltpu.VMEM((Z, SEQ, 512), BF16),
            pltpu.VMEM((2048, 1024), BF16),
            pltpu.VMEM((Z, 2 * FF, 512), BF16),
            pltpu.VMEM((2 * FF, SEQ), F32),
            pltpu.VMEM((4, 1, 256), F32),
            pltpu.VMEM((FF, SEQ), BF16),
            pltpu.VMEM((1, 128), F32),
            pltpu.VMEM((FF, 128), BF16),
            pltpu.VMEM((FF, 128), BF16),
            pltpu.SMEM((1, 2), jnp.int32),
            pltpu.SemaphoreType.DMA((N_SEND,)),
            pltpu.SemaphoreType.DMA((N_RECV,)),
            pltpu.SemaphoreType.DMA((N_LOCAL,)),
        ],
        compiler_params=pltpu.CompilerParams(
            collective_id=0, has_side_effects=True, vmem_limit_bytes=VMEM_BYTES
        ),
    )(
        queries, keys, values, spans, resid_in.reshape(4, 2, 128, D), out_weight,
        norm_gain.reshape(D // 128, 128), gate_weight.T, up_weight.T,
    )
    return resid_out, hidden.T


def solution(mesh):
    return jax.shard_map(
        body,
        mesh=mesh,
        in_specs=(
            P(("dp", "ctx"), None),
            P(("dp", "ctx"), None),
            P(("dp", "ctx"), None),
            P("dp", None),
            P("dp", None),
            P("ctx", "dp"),
            P(),
            P("dp", "ctx"),
            P("dp", "ctx"),
        ),
        out_specs=(P(("dp", "ctx"), None), P("dp", "ctx")),
        check_vma=False,
    )
```

```python
import functools
import math

import jax
import jax.numpy as jnp
from jax import lax
from jax.experimental import pallas as pl
from jax.experimental.pallas import tpu as pltpu
from jax.sharding import PartitionSpec as P

MESH = pl.DeviceIdType.MESH
Z, Y, X = 8, 4, 4
HD = 128
SEQ, D, FF = 1024, 4096, 688
PART_ROWS = {"A": (0, 448), "B": (448, 2 * FF - 448)}
EXP2_SCALE = math.log2(math.e) / math.sqrt(HD)
F32, BF16 = jnp.float32, jnp.bfloat16
VMEM_BYTES = 56 * 1024 * 1024
N_SEND, N_RECV, N_LOCAL = 11, 74, 9


def mult(value, of):
    return pl.multiple_of(value, of)


def kernel(
    q_in, k_in, v_in, spans_in, resid, wo_in, gain_in, gate_hbm, up_hbm,
    resid_out, hidden,
    qkv, ctx_own, ctx_all, res, stream, wo, w, acc, scales, hid, gain, gate_in, up_in, spans,
    send_sem, recv_sem, local_sem,
):
    cx, dp = lax.axis_index("ctx"), lax.axis_index("dp")
    x, c = cx // 2, cx % 2
    z, y = dp // Y, dp % Y

    def dev(dz=0, dy=0, dx=0, dc=0):
        zz, yy = (z + dz + Z) % Z, (y + dy + Y) % Y
        xx, cc = (x + dx + X) % X, (c + dc) % 2
        return (zz * Y + yy, xx * 2 + cc)

    send_ids, recv_ids, local_ids = {}, {}, {}

    def remote(src, dst, target, kind, event):
        return pltpu.make_async_remote_copy(
            src_ref=src, dst_ref=dst, send_sem=send_sem.at[send_ids.setdefault(kind, len(send_ids))],
            recv_sem=recv_sem.at[recv_ids.setdefault(event, len(recv_ids))], device_id=target, device_id_type=MESH,
        )

    def send(src, dst, target, kind, event):
        remote(src, dst, target, kind, event).start()

    def recv(as_large, event):
        remote(as_large, as_large, dev(0, 0, 0, 1), "qkv", event).wait_recv()

    def sent(as_large, kind):
        remote(as_large, as_large, dev(0, 0, 0, 1), kind, "q").wait_send()

    def local(src, dst, kind):
        index = local_ids.setdefault(kind, len(local_ids))
        pltpu.make_async_copy(src, dst, local_sem.at[index]).start()

    def local_wait(as_large, kind):
        pltpu.make_async_copy(as_large, as_large, local_sem.at[local_ids[kind]]).wait()

    def wo_block(zz, cc, unit=None):
        rows = pl.ds(mult(cc * 1024, 1024), 1024) if unit is None else pl.ds(mult(cc * 1024 + unit * 512, 512), 512)
        return wo.at[rows, pl.ds(mult((zz + Z) % Z * 128, 128), 128)]

    def wo_rows(xx):
        return wo.at[pl.ds(mult(c * 1024 + xx * 256, 256), 256), pl.ds(mult(z * 128, 128), 128)]

    ahead = (y - x + X) % X
    collector = ahead == 0

    @pl.when(collector)
    def _():
        local(wo_in, wo_rows(x), "wo")

    local(gate_hbm, gate_in, "gate")
    local(up_hbm, up_in, "up")
    local(gain_in.at[pl.ds(dp, 1), :], gain, "gain")
    local(spans_in, spans, "spans")

    barrier = pltpu.get_barrier_semaphore()
    peers = [(0, 0, dx, dc) for dx in range(X) for dc in range(2) if (dx, dc) != (0, 0)]
    peers += [(0, 1, 0, 0), (0, 2, 0, 0), (0, 3, 0, 0), (1, 0, 0, 0), (-1, 0, 0, 0)]
    for peer in peers:
        pl.semaphore_signal(barrier, inc=1, device_id=dev(*peer), device_id_type=MESH)


    def pack_own():
        local_wait(gate_in, "gate")
        local_wait(up_in, "up")
        local_wait(gain, "gain")
        gain_row = gain[...]
        columns = pl.ds(mult(y * 128, 128), 128)
        w[z, :FF, columns] = (gate_in[...].astype(F32) * gain_row).astype(BF16)
        w[z, FF:, columns] = (up_in[...].astype(F32) * gain_row).astype(BF16)

    pack_own()
    pl.semaphore_wait(barrier, len(peers))

    @pl.when(jnp.logical_not(collector))
    def _():
        for piece in range(4):
            rows = pl.ds(mult(c * 1024 + x * 256 + piece * 64, 64), 64)
            target = wo.at[rows, pl.ds(mult(z * 128, 128), 128)]
            send(wo_in.at[64 * piece : 64 * piece + 64, :], target, dev(0, 0, ahead, 0), "wo_x", "wo_x")

    def w_block(part, dz, dy, half=None):
        first, count = PART_ROWS[part]
        if half is not None:
            first, count = first + half * count // 2, count // 2
        return w.at[(z + dz + Z) % Z, first : first + count, pl.ds(mult((y + dy + Y) % Y * 128, 128), 128)]

    def w_like(part, z_blocks, y_blocks):
        first, count = PART_ROWS[part]
        return w.at[:z_blocks, first : first + count, : 128 * y_blocks]

    def z_send(part, dz, dy, d, hop, half=None):
        ref = w_block(part, dz, dy, half)
        send(ref, ref, dev(d, 0, 0, 0), (part, "z"), (part, "z", dy, hop))

    def y_send(part, dz, dy, d, hop, half=None):
        ref = w_block(part, dz, dy, half)
        send(ref, ref, dev(0, d, 0, 0), (part, "y"), (part, "y", dz, hop))

    def z_start(part, dy):
        for d in (1, -1):
            z_send(part, 0, dy, d, 1)

    def z_wait(part, dy, hop):
        recv(w_like(part, 2 if hop < 4 else 1, 1), (part, "z", dy, hop))

    def z_pass(part, dy, hop):
        for d in (1, -1):
            half = None if hop < 3 else (0 if d == 1 else 1)
            z_send(part, -d * hop, dy, d, hop + 1, half)

    def z_event(part, dy, hop):
        z_wait(part, dy, hop)
        if hop < 4:
            z_pass(part, dy, hop)

    def y_start(part, dz):
        for d in (1, -1):
            y_send(part, dz, 0, d, 1)

    def y_event(part, dz, hop):
        recv(w_like(part, 2 if hop < 2 else 1, 1), (part, "y", dz, hop))
        if hop == 1:
            for d in (1, -1):
                y_send(part, dz, -d, d, 2, 0 if d == 1 else 1)

    y_start("A", 0)
    z_start("B", 0)
    z_start("A", 0)

    @pl.when(jnp.logical_not(collector))
    def _():
        y_start("B", 0)

    mine = pl.ds(mult(cx * 128, 128), 128)
    shares = {"k": (1, k_in), "v": (2, v_in), "q": (0, q_in)}

    def share(name):
        which, source = shares[name]
        for dx, dc in [(0, 1), (2, 0), (2, 1), (1, 0), (1, 1), (3, 0), (3, 1)]:
            target = dev(0, 0, dx, dc)
            columns = pl.ds(mult(target[1] * 256, 256), 256)
            event = "sibling" if dx == 0 and name == "k" else name
            send(source.at[:, columns], qkv.at[which, mine], target, "qkv", event)
            if event == "sibling":
                recv(qkv.at[0, :128], event)
        local(source.at[:, pl.ds(mult(cx * 256, 256), 256)], qkv.at[which, mine], "qkv")

    share("k")

    def wo_along_y(unit, d):
        ref = wo_block(z, c, unit)
        send(ref, ref, dev(0, d, 0, 0), "wo_y", ("wo_y", unit))

    @pl.when(collector)
    def _():
        recv(wo.at[:256, :384], "wo_x")
        local_wait(wo_rows(x), "wo")
        wo_along_y(0, 1)
        wo_along_y(1, -1)

    def wo_y_wait(unit):
        @pl.when(jnp.logical_not(collector))
        def _():
            recv(wo_block(z, c, unit), ("wo_y", unit))

        d = 1 if unit == 0 else -1

        @pl.when(ahead == d % Y)
        def _():
            wo_along_y(unit, d)

    def wo_across(dz, unit):
        ref = wo_block(z + dz, c, unit)
        send(ref, ref, dev(0, 0, 0, 1), "wo_d", "wo_d")

    def wo_start(unit):
        ref = wo_block(z, c, unit)
        for d in (1, -1):
            send(ref, ref, dev(d, 0, 0, 0), "wo_z", ("wo_z", unit, 1))
        wo_across(0, unit)

    def wo_event(unit, hop):
        recv(wo_block(0, 0, 0) if hop == 4 else wo.at[:512, :256], ("wo_z", unit, hop))
        for d in (1, -1):
            if hop == 4 and unit != (0 if d == 1 else 1):
                continue
            ref = wo_block(z - d * hop, c, unit)
            if hop < 3 or (hop == 3 and unit == (0 if d == 1 else 1)):
                send(ref, ref, dev(d, 0, 0, 0), "wo_z", ("wo_z", unit, hop + 1))
            wo_across(4 if hop == 4 else -d * hop, unit)

    def wo_d_wait():
        recv(wo.at[:1024, :], "wo_d")

    def qkv_wait():
        local_wait(qkv.at[:, :128, :], "qkv")
        for name in shares:
            recv(qkv.at[0, : 768 if name == "k" else 896], name)

    local_wait(spans, "spans")
    prefix_end, middle_end = spans[0, 0], spans[0, 1]

    def ranks(pos):
        late = prefix_end + (SEQ - middle_end) + (pos - prefix_end)
        return jnp.where(pos < prefix_end, pos, jnp.where(pos >= middle_end, prefix_end + pos - middle_end, late))

    key_rank = ranks(lax.broadcasted_iota(jnp.int32, (1, SEQ), 1))

    def ctx_spot(k, cc, xx, half=None):
        rows = pl.ds(128 * k, 128) if half is None else pl.ds(128 * k + 64 * half, 64)
        return ctx_all.at[rows, pl.ds(mult(cc * 1024 + xx * 256, 256), 256)]

    def attend(k, rel):
        row = mult((2 * k + (c + rel) % 2) * 128, 128)
        rows = pl.ds(row, 128)
        query_rank = ranks(row + lax.broadcasted_iota(jnp.int32, (128, 1), 0))
        allowed = query_rank >= key_rank
        for head in range(2):
            cols = slice(head * HD, head * HD + HD)
            scores = lax.dot_general(
                qkv[0, rows, cols], qkv[1, :, cols], (((1,), (1,)), ((), ())), preferred_element_type=F32
            )
            scores = jnp.where(allowed, scores, -jnp.inf)
            peak = jnp.max(scores, axis=1, keepdims=True)
            expo = jnp.exp2((scores - peak) * EXP2_SCALE)
            total = jnp.sum(expo, axis=1, keepdims=True)
            mixed = jnp.dot(expo.astype(BF16), qkv[2, :, cols], preferred_element_type=F32)
            mixed = (mixed / total).astype(BF16)
            ctx_own[rows, cols] = mixed
            if rel == 0:
                ctx_all[128 * k : 128 * k + 128, pl.ds(mult(c * 1024 + x * 256 + head * HD, 128), HD)] = mixed
        for d in (1, -1):
            send(ctx_own.at[rows], ctx_spot(k, c, x), dev(0, 0, d, rel), "ctx", ("ctx", k, 1))
        if rel == 1:
            send(ctx_own.at[rows], ctx_spot(k, c, x), dev(0, 0, 0, 1), "ctx", ("ctx", k, 2))

    def ctx_pass(k):
        recv(ctx_all.at[:128, :1024], ("ctx", k, 1))
        for rel in range(2):
            for d in (1, -1):
                ref = ctx_spot(k, (c + rel) % 2, (x - d + X) % X, 0 if d == 1 else 1)
                send(ref, ref, dev(0, 0, d, 0), "ctx", ("ctx", k, 2))

    def ctx_end(k):
        recv(ctx_all.at[:128, :768], ("ctx", k, 2))

    for zz in range(Z):
        columns = pl.ds(mult(zz * 512 + x * 128, 128), 128)
        local(resid.at[:, c, :, columns], res.at[:, :, 128 * zz : 128 * zz + 128], "res")

    def stream_spot(k, cc, xx, half=None):
        row = (2 * k + cc) * 128
        rows = pl.ds(mult(row, 128), 128) if half is None else pl.ds(mult(row + half * 64, 64), 64)
        return stream.at[:, rows, pl.ds(mult(xx * 128, 128), 128)]

    def project(k):
        rows = pl.ds(mult((2 * k + c) * 128, 128), 128)
        columns = pl.ds(mult(x * 128, 128), 128)
        for block in range(4):
            part = jnp.dot(
                ctx_all[128 * k : 128 * k + 128, :], wo[:, 256 * block : 256 * block + 256], preferred_element_type=F32
            )
            part = part + res[k, :, 256 * block : 256 * block + 256].astype(F32)
            stream[2 * block, rows, columns] = part[:, :128].astype(BF16)
            stream[2 * block + 1, rows, columns] = part[:, 128:].astype(BF16)
        ref = stream_spot(k, c, x)
        for d in (1, -1):
            send(ref, ref, dev(0, 0, d, 0), "stream", ("stream", k, 1))
        send(ref, ref, dev(0, 0, 0, 1), "stream", ("across", k))

    def stream_pass(k, hop):
        recv(stream.at[:, : 256 // hop, :128], ("stream", k, hop))
        for d in (1, -1):
            half = 0 if d == 1 else 1
            if hop == 1:
                ref = stream_spot(k, c, (x - d + X) % X, half)
                send(ref, ref, dev(0, 0, d, 0), "stream", ("stream", k, 2))
            ref = stream_spot(k, c, (x - d * hop + X) % X, None if hop == 1 else half)
            send(ref, ref, dev(0, 0, 0, 1), "stream", ("across", k))

    def stream_end(k):
        recv(stream.at[:, :128, :], ("across", k))

    def norm_scale(k):
        rows = pl.ds(256 * k, 256)

        def add_squares(i, total):
            piece = stream[i, rows, :].astype(F32)
            piece = piece * piece
            return total + (piece[:, :128] + piece[:, 128:256]) + (piece[:, 256:384] + piece[:, 384:])

        squares = lax.fori_loop(0, Z, add_squares, jnp.zeros((256, 128), F32))
        total = jnp.sum(squares.T, axis=0, keepdims=True)
        scales[k] = lax.rsqrt(total * (1.0 / D) + 1e-5)

    def ff_part(k, *dzs):
        rows = slice(256 * k, 256 * k + 256)

        def one(half, _):
            at = pl.ds(mult(half * FF, 16), FF)
            total = None
            for dz in dzs:
                zz = (z + dz + Z) % Z
                part = lax.dot_general(
                    w[zz, at, :], stream[zz, rows, :], (((1,), (1,)), ((), ())), preferred_element_type=F32
                )
                total = part if total is None else total + part
            acc[at, rows] = total if 0 in dzs else acc[at, rows] + total
            return 0

        lax.fori_loop(0, 2, one, 0)

    def activate(k):
        rows = slice(256 * k, 256 * k + 256)
        scale = scales[k]
        for first in range(0, FF, 128):
            count = min(128, FF - first)
            gate = acc[first : first + count, rows] * scale
            up = acc[FF + first : FF + first + count, rows] * scale
            hid[first : first + count, rows] = (gate / (1.0 + jnp.exp(-gate)) * up).astype(BF16)
            if first in (256, 640):
                done = slice(0, 384) if first == 256 else slice(384, FF)
                local(hid.at[done, rows], hidden.at[done, rows], "hidden")

    y_event("A", 0, 1)
    share("v")
    share("q")

    def fill_z():
        z_start("A", -1)
        z_pass("B", 0, 1)

    z_wait("B", 0, 1)

    @pl.when(collector)
    def _():
        wo_along_y(1, 1)
        wo_along_y(0, -1)

    @pl.when(jnp.logical_not(collector))
    def _():
        fill_z()

    def next_y():
        y_start("B", 1)
        y_start("B", -1)

    @pl.when(ahead == 2)
    def _():
        next_y()

    def wo_units(*units):
        for unit in units:
            wo_y_wait(unit)
            wo_start(unit)

    @pl.when(ahead == 3)
    def _():
        wo_units(1, 0)

    @pl.when(ahead != 3)
    def _():
        wo_units(0, 1)

    @pl.when(collector)
    def _():
        wo_event(0, 1)
        y_start("B", 0)
        wo_event(1, 1)
        fill_z()

    @pl.when(collector)
    def _():
        next_y()

    qkv_wait()

    @pl.when(ahead % 2 == 1)
    def _():
        next_y()

    attend(0, 1)
    attend(0, 0)

    @pl.when(jnp.logical_not(collector))
    def _():
        wo_event(0, 1)

    attend(1, 1)
    attend(1, 0)

    @pl.when(jnp.logical_not(collector))
    def _():
        wo_event(1, 1)

    y_event("B", 0, 1)
    attend(2, 1)
    attend(2, 0)
    wo_event(0, 2)
    attend(3, 1)
    attend(3, 0)
    wo_event(1, 2)
    z_wait("B", 0, 2)
    y_start("B", 2)
    y_start("B", -2)
    ctx_pass(0)
    wo_event(0, 3)
    ctx_pass(1)
    y_event("A", 0, 2)
    wo_event(1, 3)
    ctx_pass(2)
    y_event("B", -1, 1)
    y_event("B", 1, 1)
    wo_event(0, 4)
    z_pass("B", 0, 2)
    wo_event(1, 4)
    z_event("A", 0, 1)
    z_start("A", 1)
    z_start("A", 2)
    ctx_pass(3)
    local_wait(res, "res")
    wo_d_wait()
    ctx_end(0)
    project(0)
    z_event("A", -1, 1)
    ctx_end(1)
    project(1)
    z_event("B", 0, 3)
    y_start("B", 3)
    y_start("B", -3)
    stream_pass(0, 1)
    ctx_end(2)
    project(2)
    y_event("B", 2, 1)
    y_event("B", -2, 1)
    z_event("A", 0, 2)
    z_event("A", 1, 1)
    z_event("A", 2, 1)
    z_event("A", -1, 2)
    stream_pass(1, 1)
    ctx_end(3)
    project(3)
    z_event("B", 0, 4)
    y_start("B", 4)
    stream_pass(0, 2)
    stream_end(0)
    norm_scale(0)
    y_event("B", 0, 2)
    y_event("B", -1, 2)
    y_event("B", 1, 2)
    ff_part(0, 0, 1, -1)
    stream_pass(2, 1)
    y_event("B", 3, 1)
    y_event("B", -3, 1)
    stream_pass(1, 2)
    z_event("A", 0, 3)
    z_event("A", 1, 2)
    z_event("A", 2, 2)
    z_event("A", -1, 3)
    y_event("B", 2, 2)
    y_event("B", -2, 2)
    ff_part(0, 2, -2)
    stream_end(1)
    norm_scale(1)
    ff_part(1, 0, 1, -1)
    stream_pass(3, 1)
    y_event("B", 4, 1)
    z_event("A", 1, 3)
    ff_part(1, 2, -2)
    stream_pass(2, 2)
    z_event("A", 2, 3)
    y_event("B", 3, 2)
    y_event("B", -3, 2)
    ff_part(0, 3, -3)
    stream_pass(3, 2)
    ff_part(1, 3, -3)
    stream_end(2)
    norm_scale(2)
    stream_end(3)
    for zz in range(Z):
        local(stream.at[zz, mine, :], resid_out.at[:, 512 * zz : 512 * zz + 512], "resid_out")
    norm_scale(3)

    def early_sent():
        @pl.when(jnp.logical_not(collector))
        def _():
            sent(wo_in, "wo_x")

        @pl.when(collector)
        def _():
            sent(wo.at[:512, :512], "wo_y")

        @pl.when(ahead % 2 == 1)
        def _():
            sent(wo_block(0, 0, 0), "wo_y")

        sent(wo.at[:1024, :896], "wo_z")
        sent(wo.at[:1024, :], "wo_d")
        sent(qkv.at[:, :896], "qkv")
        sent(ctx_all.at[:448, :], "ctx")
        sent(stream.at[:, :896, :], "stream")
        sent(w_like("A", 3, 1), ("A", "y"))

    early_sent()
    for dy in (0, -1, 1, 2):
        z_event("A", dy, 4)
    y_event("B", 4, 2)
    ff_part(2, 0, 1, -1, 2, -2, 3, -3, 4)
    activate(2)
    for k in range(2):
        ff_part(k, 4)
        activate(k)
    ff_part(3, 0, 1, -1, 2, -2, 3, -3, 4)
    activate(3)
    sent(w_like("A", 7, 4), ("A", "z"))
    sent(w_like("B", 7, 1), ("B", "z"))
    sent(w_like("B", 6, 4), ("B", "y"))
    local_wait(stream.at[:4, :256, :], "resid_out")
    local_wait(hid, "hidden")
    assert (len(send_ids), len(recv_ids), len(local_ids)) == (N_SEND, N_RECV, N_LOCAL), (send_ids, recv_ids, local_ids)


def body(queries, keys, values, spans, resid_in, out_weight, norm_gain, gate_weight, up_weight):
    anywhere = pl.BlockSpec(memory_space=pl.ANY)
    resid_out, hidden = pl.pallas_call(
        kernel,
        out_shape=(jax.ShapeDtypeStruct((128, D), BF16), jax.ShapeDtypeStruct((FF, SEQ), BF16)),
        in_specs=[pl.BlockSpec(memory_space=pltpu.HBM)] * 9,
        out_specs=(anywhere, anywhere),
        scratch_shapes=[
            pltpu.VMEM((3, SEQ, 256), BF16),
            pltpu.VMEM((SEQ, 256), BF16),
            pltpu.VMEM((512, 2048), BF16),
            pltpu.VMEM((4, 128, 1024), BF16),
            pltpu.VMEM((Z, SEQ, 512), BF16),
            pltpu.VMEM((2048, 1024), BF16),
            pltpu.VMEM((Z, 2 * FF, 512), BF16),
            pltpu.VMEM((2 * FF, SEQ), F32),
            pltpu.VMEM((4, 1, 256), F32),
            pltpu.VMEM((FF, SEQ), BF16),
            pltpu.VMEM((1, 128), F32),
            pltpu.VMEM((FF, 128), BF16),
            pltpu.VMEM((FF, 128), BF16),
            pltpu.SMEM((1, 2), jnp.int32),
            pltpu.SemaphoreType.DMA((N_SEND,)),
            pltpu.SemaphoreType.DMA((N_RECV,)),
            pltpu.SemaphoreType.DMA((N_LOCAL,)),
        ],
        compiler_params=pltpu.CompilerParams(
            collective_id=0, has_side_effects=True, vmem_limit_bytes=VMEM_BYTES
        ),
    )(
        queries, keys, values, spans, resid_in.reshape(4, 2, 128, D), out_weight,
        norm_gain.reshape(D // 128, 128), gate_weight.T, up_weight.T,
    )
    return resid_out, hidden.T


def solution(mesh):
    return jax.shard_map(
        body,
        mesh=mesh,
        in_specs=(
            P(("dp", "ctx"), None),
            P(("dp", "ctx"), None),
            P(("dp", "ctx"), None),
            P("dp", None),
            P("dp", None),
            P("ctx", "dp"),
            P(),
            P("dp", "ctx"),
            P("dp", "ctx"),
        ),
        out_specs=(P(("dp", "ctx"), None), P("dp", "ctx")),
        check_vma=False,
    )
```
